32 devices in a mesh: dp: 4 (over y, x), fsdp: 8 (over z, core).
Axes of the slice: x: 2, y: 2, z: 4, core: 2. Of those that a mesh axis runs over, the one named last changes fastest.
Arguments:
- hidden: bfloat16 [32, 256, 5120], P(('dp', 'fsdp')), may hold values from -6 to 6
- queries: bfloat16 [32, 256, 1024], P(('dp', 'fsdp')), may hold values from -6 to 6
- upstream: bfloat16 [32, 256, 1024], P(('dp', 'fsdp')), may hold values from -0.3984375 to 0.3984375
- advantage: float32 [32, 256], P(('dp', 'fsdp')), may hold values from -5 to 5
- selected: int32 [32, 256], P(('dp', 'fsdp')), may hold values from 0 to 1, as said below
- segment: int32 [32, 256], P(('dp', 'fsdp')), may hold values from 0 to 3, never falling along the last dimension, each value on 1 to 128 neighbouring positions
- w_kv: bfloat16 [5120, 256], P('fsdp'), may hold values from -0.078125 to 0.078125
- k_gain: float32 [128], replicated, may hold values from 0.25 to 1.75
- q_gain: float32 [128], replicated, may hold values from 0.25 to 1.75
Outputs:
- d_weight: float32 [5120, 256], P('fsdp')
- d_gain: float32 [128], replicated
The draws below stay inside these ranges and needn't reach their ends.
Inputs may be any that keep to these rules, and one draw needn't show every extreme that they name: Each row has at most 128 selected tokens, and some row has exactly 128.
All inputs are finite; a program needn't handle non-finite values.
Results may differ from the reference program's by a relative error of at most 0.007.
Values may be sent and summed in bfloat16 or wider, within the bound.
A program may use at most 64 MiB of HBM per device.

```python
import math
import jax
import jax.numpy as jnp
import numpy as np
from jax import lax

D = 5120
GROUP = 8
HD = 128
TOK_DEV = 256
SEGS = 4
CAP = 128
ROWS = 32
D_PAD = 5120


def draw_selected(key, part):
    key_count = jax.random.fold_in(key, 101)
    key_top = jax.random.fold_in(key, 202)
    key_order = jax.random.fold_in(key, 303)
    spread = jax.random.randint(key_count, (ROWS,), 0, CAP)
    counts = 1 + spread * (spread + CAP) // (2 * CAP)
    busiest = jax.random.randint(key_top, (), 0, ROWS)
    counts = jnp.where(jnp.arange(ROWS) == busiest, CAP, counts)
    row_keys = jax.random.split(key_order, ROWS)
    orders = jax.vmap(lambda one_key: jax.random.permutation(one_key, TOK_DEV))(row_keys)
    ranks = jnp.argsort(orders, axis=1, stable=True)
    return (ranks < counts[:, None]).astype(jnp.int32)


def with_spikes(array, key, source, target, shards_of, factor):
    def block_of(position):
        return (jnp.arange(array.shape[position]) // (array.shape[position] // shards_of)).reshape((-1,) + (1,) * (array.ndim - 1 - position))

    near = jax.random.permutation(key, shards_of)[block_of(target)]
    second = (block_of(target) + shards_of // 2) % shards_of
    return jnp.where((block_of(source) == near) | (block_of(source) == second), factor * array, array)


def shard_levels(own_key, extent, cuts, least, top_value):
    level, own = 1.0, jax.random.fold_in(own_key, 6)
    for dim, blocks in cuts:
        heights = jnp.exp(jax.random.uniform(jax.random.fold_in(own, dim), (blocks,), jnp.float32, least / len(cuts), top_value / len(cuts)))
        level = level * jnp.repeat(heights, extent[dim] // blocks).reshape([-1 if axis == dim else 1 for axis in range(len(extent))])
    return level


def split_up(number_of, total, bound, skew):
    weights = [(1 << 20) // math.isqrt(standing ** skew) + 1 for standing in range(2, number_of + 1)]
    surplus, given = total - bound - (number_of - 1), [1] * (number_of - 1)
    while surplus > 0:
        movable = [i for i in range(number_of - 1) if given[i] < bound]
        whole, budget = sum([weights[i] for i in movable]), surplus
        for i in movable:
            extra = min(bound - given[i], max(1, budget * weights[i] // whole), surplus)
            given[i] = given[i] + extra
            surplus = surplus - extra
    return np.array([bound] + given)


def ragged(stream_key, amount, total, bound, lean):
    if amount == 2:
        one = jax.random.randint(stream_key, (), max(1, total - bound), min(bound, total - 1) + 1)
        return jnp.stack([one, total - one])
    tallies = jnp.asarray(split_up(amount, total, bound, lean), jnp.int32)
    twos = (amount - 1) // 2
    donor, sink = tallies[1:1 + 2 * twos:2], tallies[2:2 + 2 * twos:2]
    room = jnp.minimum(donor - 1, bound - sink)
    shifted = jax.random.randint(jax.random.fold_in(stream_key, 1), (twos,), 0, 1 << 20) % (room + 1)
    tallies = tallies.at[1:1 + 2 * twos:2].set(donor - shifted).at[2:2 + 2 * twos:2].set(sink + shifted)
    return tallies[jax.random.permutation(jax.random.fold_in(stream_key, 2), amount)]


def normal_values(stream_key, dims, scale, most, pieces=(), kind=jnp.bfloat16):
    drawn = jax.random.normal(stream_key, dims, jnp.float32) * scale
    if len(pieces) > 0:
        drawn = shard_levels(stream_key, dims, pieces, -0.22, 0.18) * drawn
    return jnp.clip(drawn, min=-most, max=most).astype(kind)


def gaussian_with(rng, extent, scale, most, shards, heavy, kind=jnp.bfloat16):
    values = scale * jax.random.normal(rng, extent, jnp.float32)
    if shards:
        values = values * shard_levels(rng, extent, shards, -0.22, 0.18)
    return jnp.clip(with_spikes(values, jax.random.fold_in(rng, 3), *heavy), -most, most).astype(kind)


def setup_inputs(seed: int = 0) -> dict:
    streams_of = jax.random.split(jax.random.key(seed), 10)
    hidden = gaussian_with(streams_of[0], (ROWS, TOK_DEV, D), 1.0, 6.0, ((0, 32),), (0, 2, 32, 2.75))
    queries = normal_values(streams_of[1], (ROWS, TOK_DEV, GROUP * HD), 1.0, 6.0, ((0, 32),))
    upstream = normal_values(streams_of[2], (ROWS, TOK_DEV, GROUP * HD), 0.05, 0.3984375, ((0, 32),))
    advantage = normal_values(streams_of[3], (ROWS, TOK_DEV), 1.0, 5.0, ((0, 32),), jnp.float32)
    selected = draw_selected(jax.random.fold_in(streams_of[9], 71), 0)
    segment = jax.vmap(lambda own: jnp.searchsorted(jnp.cumsum(ragged(own, SEGS, TOK_DEV, TOK_DEV // 2, 1)), jnp.arange(TOK_DEV), side="right"))(jax.random.split(streams_of[5], ROWS)).reshape((ROWS, TOK_DEV)).astype(jnp.int32)
    w_kv = normal_values(streams_of[6], (D_PAD, 2 * HD), D ** -0.5, 0.078125, ((0, 8),))
    k_gain = jnp.clip(1.0 + 0.15 * jax.random.normal(streams_of[7], (HD,), jnp.float32), 0.25, 1.75)
    q_gain = jnp.clip(1.0 + 0.15 * jax.random.normal(streams_of[8], (HD,), jnp.float32), 0.25, 1.75)
    return {"hidden": hidden, "queries": queries, "upstream": upstream, "advantage": advantage, "selected": selected, "segment": segment, "w_kv": w_kv, "k_gain": k_gain, "q_gain": q_gain}


epsilon = 1e-06

def reference(hidden, queries, upstream, advantage, selected, segment, w_kv, k_gain, q_gain):
    weight = w_kv[:D]
    score_scale = HD ** (-0.5)

    def one_row(carry, inputs):
        total_w, total_g = carry
        hidden_row, query_row, upstream_row, advantage_row, selected_row, segment_row = inputs
        key_value = jnp.dot(hidden_row, weight, preferred_element_type=jnp.float32)
        k_raw = key_value[:, :HD]
        k_scale = lax.rsqrt(lax.optimization_barrier(jnp.mean(k_raw * k_raw, axis=-1, keepdims=True)) + epsilon)
        k_hat = k_raw * k_scale
        k_norm = (k_hat * k_gain).astype(jnp.bfloat16)
        values = key_value[:, HD:].astype(jnp.bfloat16)
        query_full = query_row.reshape(TOK_DEV, GROUP, HD).astype(jnp.float32)
        q_scale = lax.rsqrt(lax.optimization_barrier(jnp.mean(query_full * query_full, axis=-1, keepdims=True)) + epsilon)
        q_norm = (query_full * q_scale * q_gain).astype(jnp.bfloat16)
        token_weight = advantage_row * selected_row.astype(jnp.float32)
        cotangent = (token_weight[:, None] * upstream_row.astype(jnp.float32)).astype(jnp.bfloat16)
        cotangent = cotangent.reshape(TOK_DEV, GROUP, HD)
        positions = jnp.arange(TOK_DEV, dtype=jnp.int32)
        allowed = (segment_row[:, None] == segment_row[None, :]) & (positions[None, :] <= positions[:, None])
        scores = jnp.einsum('qhd,kd->hqk', q_norm.astype(jnp.float32), k_norm.astype(jnp.float32)) * score_scale
        expo = jnp.where(allowed[None], jnp.exp(scores), 0.0)
        probs = expo / lax.optimization_barrier(jnp.sum(expo, axis=-1, keepdims=True))
        probs_b = probs.astype(jnp.bfloat16)
        outputs = jnp.einsum('hqk,kd->qhd', probs_b.astype(jnp.float32), values.astype(jnp.float32))
        delta = lax.optimization_barrier(jnp.sum(cotangent.astype(jnp.float32) * outputs, axis=-1))
        dprob = jnp.einsum('qhd,kd->hqk', cotangent.astype(jnp.float32), values.astype(jnp.float32))
        dscore = (probs * (dprob - delta.T[:, :, None]) * score_scale).astype(jnp.bfloat16)
        d_key = jnp.einsum('hqk,qhd->kd', dscore.astype(jnp.float32), q_norm.astype(jnp.float32))
        d_value = jnp.einsum('hqk,qhd->kd', probs_b.astype(jnp.float32), cotangent.astype(jnp.float32))
        d_khat = d_key * k_gain
        gain_term = lax.optimization_barrier(jnp.sum(d_key * k_hat, axis=0))
        d_kraw = k_scale * (d_khat - k_hat * lax.optimization_barrier(jnp.mean(d_khat * k_hat, axis=-1, keepdims=True)))
        d_kv = jnp.concatenate([d_kraw, d_value], axis=1).astype(jnp.bfloat16)
        total_w = total_w + jnp.dot(hidden_row.T, d_kv, preferred_element_type=jnp.float32)
        return ((total_w, total_g + gain_term), None)
    start = (jnp.zeros((D, 2 * HD), jnp.float32), jnp.zeros((HD,), jnp.float32))
    (total_w, total_g), _ = lax.scan(one_row, start, (hidden, queries, upstream, advantage, selected, segment))
    d_weight = jnp.concatenate([total_w, jnp.zeros((D_PAD - D, 2 * HD), jnp.float32)], axis=0)
    return (d_weight, total_g)
```

```python
import functools
import math

import jax
import jax.numpy as jnp
from jax import lax
from jax.experimental import pallas as pl
from jax.experimental.pallas import tpu as pltpu
from jax.sharding import PartitionSpec as P

CAP = 128
epsilon = 1e-06
MESH = pl.DeviceIdType.MESH
F32 = jnp.float32
BF16 = jnp.bfloat16


def dot_last(a, b):
    return lax.dot_general(a, b, (((1,), (1,)), ((), ())), preferred_element_type=F32)


def dot(a, b):
    return jnp.dot(a, b, preferred_element_type=F32)


def body(
    data,
    owners,
    hidden,
    queries,
    upstream,
    advantage,
    selected,
    segment,
    w_own,
    k_gain,
    q_gain,
    d_weight,
    d_gain,
    hid,
    hid_t,
    w_half,
    q_raw,
    u_raw,
    q_sel,
    c_sel,
    allowed,
    kv_out,
    kv_in,
    d_kv,
    part,
    from_data,
    z_out,
    from_z,
    final,
    gain_core,
    gain_data,
    gain_z,
    local_sem,
    hid_sem,
    w_z_sem,
    w_data_sem,
    core_sem,
    part_sem,
    z_sem,
    final_sem,
    gain_data_sem,
    gain_z_sem,
):
    chips = owners // 2
    rows = w_own.shape[0]
    share = rows // data
    length = hidden.shape[0]
    head_dim = k_gain.shape[1]
    heads = queries.shape[1] // head_dim
    cap = allowed.shape[1] // 2
    scale = head_dim ** (-0.5)
    dp = lax.axis_index("dp")
    me = lax.axis_index("fsdp")
    chip = me // 2
    core = me % 2
    sibling = {"dp": dp, "fsdp": chip * 2 + 1 - core}

    def chip_at(k):
        return lax.rem(chip + k, chips)

    def data_at(k):
        return lax.rem(dp + k, data)

    def to_chip(other):
        return {"dp": dp, "fsdp": other * 2 + core}

    def to_data(other):
        return {"dp": other, "fsdp": me}

    def rows_of(p):
        return pl.ds(pl.multiple_of(p * share, 16), share)

    def remote(src, dst, send, recv, device):
        return pltpu.make_async_remote_copy(
            src_ref=src, dst_ref=dst, send_sem=send, recv_sem=recv, device_id=device, device_id_type=MESH
        )

    own_w = pltpu.make_async_copy(w_own, w_half.at[chip], local_sem.at[0])
    own_w.start()
    load_q = pltpu.make_async_copy(queries, q_raw, local_sem.at[1])
    load_q.start()
    load_u = pltpu.make_async_copy(upstream, u_raw, local_sem.at[2])
    load_u.start()
    loads = []
    for j in range(chips):
        cols = pl.ds(pl.multiple_of((2 * j + core) * rows, 128), rows)
        load = pltpu.make_async_copy(
            hidden.at[:, cols], hid.at[0, :, pl.ds(j * rows, rows)], hid_sem.at[0, j]
        )
        load.start()
        loads.append(load)

    barrier = pltpu.get_barrier_semaphore()
    pl.semaphore_signal(barrier, inc=1, device_id=sibling, device_id_type=MESH)
    for k in range(1, chips):
        pl.semaphore_signal(barrier, inc=1, device_id=to_chip(chip_at(k)), device_id_type=MESH)
    for k in range(1, data):
        pl.semaphore_signal(barrier, inc=1, device_id=to_data(data_at(k)), device_id_type=MESH)
    pl.semaphore_wait(barrier, chips + data - 1)

    mine = rows_of(dp)
    sends = []
    for k in range(1, chips):
        copy = remote(
            w_own.at[mine], w_half.at[chip, mine], w_z_sem.at[0, k], w_z_sem.at[1, k], to_chip(chip_at(k))
        )
        copy.start()
        sends.append(copy)
    swaps = []
    for j in range(chips):
        cols = pl.ds(pl.multiple_of((2 * j + 1 - core) * rows, 128), rows)
        copy = remote(
            hidden.at[:, cols],
            hid.at[1, :, pl.ds(j * rows, rows)],
            hid_sem.at[1, j],
            hid_sem.at[2, j],
            sibling,
        )
        copy.start()
        swaps.append(copy)

    chosen = selected[...].astype(F32)
    places = lax.broadcasted_iota(jnp.int32, (length, length), 0)
    others = lax.broadcasted_iota(jnp.int32, (length, length), 1)
    upto = places <= others
    rank = dot(jnp.broadcast_to(chosen, (16, length)).astype(BF16), upto.astype(F32).astype(BF16))[:1]
    slots = lax.broadcasted_iota(jnp.int32, (cap, length), 0).astype(F32) + 1.0
    pick = jnp.where(rank == slots, chosen, 0.0)
    pick_b = pick.astype(BF16)
    token_weight = jnp.sum(pick * (advantage[...] * chosen), axis=1, keepdims=True)
    groups = jnp.broadcast_to(segment[...].astype(F32), (length, length))
    allowed_full = jnp.where((groups == groups.T) & upto, 1.0, 0.0).astype(BF16)
    allowed_sel = dot_last(allowed_full, pick_b)
    allowed[:, :cap] = allowed_sel
    allowed[:, cap:] = allowed_sel

    def forward(k):
        sends[k - 1].wait_recv()
        source = chip_at(chips - k)
        for d in range(1, data):
            copy = remote(
                w_half.at[source, mine],
                w_half.at[source, mine],
                w_data_sem.at[0, k, d],
                w_data_sem.at[1, k, d],
                to_data(data_at(d)),
            )
            copy.start()
            forwards.append(copy)

    forwards = []
    for k in range(1, chips):
        forward(k)

    load_q.wait()
    load_u.wait()
    for h in range(heads):
        lanes = pl.ds(h * head_dim, head_dim)
        query = dot(pick_b, q_raw[:, lanes])
        query_scale = lax.rsqrt(jnp.mean(query * query, axis=-1, keepdims=True) + epsilon)
        q_sel[pl.ds(h * cap, cap)] = (query * query_scale * q_gain[...]).astype(BF16)
        grad = dot(pick_b, u_raw[:, lanes])
        c_sel[pl.ds(h * cap, cap)] = (token_weight * grad).astype(BF16)

    for j in range(chips):
        loads[j].wait()
        hid_t[pl.ds(j * rows, rows), :length] = hid[0, :, pl.ds(j * rows, rows)].T
    for j in range(chips):
        swaps[j].wait()
        hid_t[pl.ds(j * rows, rows), length:] = hid[1, :, pl.ds(j * rows, rows)].T

    own_w.wait()
    for copy in forwards:
        copy.wait_recv()

    weight = w_half[...].reshape(chips * rows, w_half.shape[2])
    kv_out[...] = dot(hid[1], weight)
    swap_kv = remote(kv_out, kv_in, core_sem.at[0], core_sem.at[1], sibling)
    swap_kv.start()
    key_value = dot(hid[0], weight)
    swap_kv.wait()
    key_value = key_value + kv_in[...]

    k_raw = key_value[:, :head_dim]
    k_scale = lax.rsqrt(jnp.mean(k_raw * k_raw, axis=-1, keepdims=True) + epsilon)
    k_hat = k_raw * k_scale
    k_norm = (k_hat * k_gain[...]).astype(BF16)
    values = key_value[:, head_dim:].astype(BF16)
    d_key = jnp.zeros((length, head_dim), F32)
    d_value = jnp.zeros((length, head_dim), F32)
    for h in range(heads // 2):
        pair = pl.ds(h * 2 * cap, 2 * cap)
        q_pair = q_sel[pair]
        c_pair = c_sel[pair]
        expo = jnp.exp(dot_last(k_norm, q_pair) * scale) * allowed[...]
        total = jnp.sum(expo, axis=0, keepdims=True)
        probs = expo * (1.0 / jnp.where(total > 0.0, total, 1.0))
        probs_b = probs.astype(BF16)
        dprob = dot_last(values, c_pair)
        delta = jnp.sum(probs_b.astype(F32) * dprob, axis=0, keepdims=True)
        dscore = (probs * (dprob - delta) * scale).astype(BF16)
        d_key += dot(dscore, q_pair)
        d_value += dot(probs_b, c_pair)
    d_khat = d_key * k_gain[...]
    d_kraw = k_scale * (d_khat - k_hat * jnp.mean(d_khat * k_hat, axis=-1, keepdims=True))
    d_kv[0, :, :head_dim] = d_kraw.astype(BF16)
    d_kv[0, :, head_dim:] = d_value.astype(BF16)
    swap_d = remote(d_kv.at[0], d_kv.at[1], core_sem.at[2], core_sem.at[3], sibling)
    swap_d.start()
    gain = jnp.sum(d_key * k_hat, axis=0, keepdims=True)
    gain_core[0] = jnp.broadcast_to(gain, (8, head_dim))
    swap_g = remote(gain_core.at[0], gain_core.at[1], core_sem.at[4], core_sem.at[5], sibling)
    swap_g.start()
    swap_d.wait()

    both = d_kv[...].reshape(2 * length, d_kv.shape[2])
    parts = []
    for k in range(1, chips + 1):
        target = chip_at(k)
        block = hid_t[pl.ds(pl.multiple_of(target * rows, 128), rows), :]
        part[target] = dot(block, both).astype(BF16)
        for d in range(1, data):
            other = data_at(d)
            copy = remote(
                part.at[target, rows_of(other)],
                from_data.at[d, target],
                part_sem.at[0, k - 1, d],
                part_sem.at[1, k - 1, d],
                to_data(other),
            )
            copy.start()
            parts.append(copy)
    swap_g.wait()
    gain_data[dp] = gain_core[0] + gain_core[1]
    gains = []
    for d in range(1, data):
        copy = remote(
            gain_data.at[dp], gain_data.at[dp], gain_data_sem.at[0, d], gain_data_sem.at[1, d], to_data(data_at(d))
        )
        copy.start()
        gains.append(copy)

    columns = []
    for k in range(1, chips + 1):
        target = chip_at(k)
        for d in range(1, data):
            parts[(k - 1) * (data - 1) + d - 1].wait_recv()
        summed = part[target, rows_of(dp)].astype(F32)
        for d in range(1, data):
            summed += from_data[d, target].astype(F32)
        if k < chips:
            z_out[k] = summed.astype(BF16)
            copy = remote(z_out.at[k], from_z.at[k], z_sem.at[0, k], z_sem.at[1, k], to_chip(target))
            copy.start()
            columns.append(copy)

    for copy in gains:
        copy.wait()
    gain_sum = gain_data[0]
    for d in range(1, data):
        gain_sum += gain_data[d]
    gain_z[chip] = gain_sum
    z_gains = []
    for k in range(1, chips):
        copy = remote(
            gain_z.at[chip], gain_z.at[chip], gain_z_sem.at[0, k], gain_z_sem.at[1, k], to_chip(chip_at(k))
        )
        copy.start()
        z_gains.append(copy)

    for k in range(1, chips):
        columns[k - 1].wait_recv()
        summed += from_z[k].astype(F32)
    final[mine] = summed.astype(BF16)
    finals = []
    for d in range(1, data):
        copy = remote(final.at[mine], final.at[mine], final_sem.at[0, d], final_sem.at[1, d], to_data(data_at(d)))
        copy.start()
        finals.append(copy)

    for copy in z_gains:
        copy.wait()
    gain_sum = gain_z[0]
    for k in range(1, chips):
        gain_sum += gain_z[k]
    d_gain[...] = gain_sum

    for copy in sends + forwards + parts + columns:
        copy.wait_send()
    for copy in finals:
        copy.wait()
    d_weight[...] = final[...].astype(F32)


def shards(data, owners, hidden, queries, upstream, advantage, selected, segment, w_kv, k_gain, q_gain):
    hidden_row = hidden[0]
    length, width = hidden_row.shape
    rows_dev, columns = w_kv.shape
    head_dim = k_gain.shape[0]
    heads = queries.shape[2] // head_dim
    unit = math.lcm(128, 16 * data)
    rows = -(-rows_dev // unit) * unit
    chips = owners // 2
    share = rows // data
    if rows_dev * owners != width:
        hidden_row = jnp.pad(hidden_row, ((0, 0), (0, rows_dev * owners - width)))
    if rows != rows_dev:
        blocks = hidden_row.reshape(length, owners, rows_dev)
        hidden_row = jnp.pad(blocks, ((0, 0), (0, 0), (0, rows - rows_dev))).reshape(length, owners * rows)
        w_kv = jnp.pad(w_kv, ((0, rows - rows_dev), (0, 0)))
    vmem = pl.BlockSpec(memory_space=pltpu.VMEM)
    hbm = pl.BlockSpec(memory_space=pl.ANY)
    dma = pltpu.SemaphoreType.DMA
    d_weight, d_gain = pl.pallas_call(
        functools.partial(body, data, owners),
        out_shape=(
            jax.ShapeDtypeStruct((rows, columns), F32),
            jax.ShapeDtypeStruct((8, head_dim), F32),
        ),
        in_specs=[hbm, hbm, hbm, vmem, vmem, vmem, hbm, vmem, vmem],
        out_specs=(vmem, vmem),
        scratch_shapes=[
            pltpu.VMEM((2, length, chips * rows), BF16),
            pltpu.VMEM((chips * rows, 2 * length), BF16),
            pltpu.VMEM((chips, rows, columns), BF16),
            pltpu.VMEM((length, heads * head_dim), BF16),
            pltpu.VMEM((length, heads * head_dim), BF16),
            pltpu.VMEM((heads * CAP, head_dim), BF16),
            pltpu.VMEM((heads * CAP, head_dim), BF16),
            pltpu.VMEM((length, 2 * CAP), F32),
            pltpu.VMEM((length, columns), F32),
            pltpu.VMEM((length, columns), F32),
            pltpu.VMEM((2, length, columns), BF16),
            pltpu.VMEM((chips, rows, columns), BF16),
            pltpu.VMEM((data, chips, share, columns), BF16),
            pltpu.VMEM((chips, share, columns), BF16),
            pltpu.VMEM((chips, share, columns), BF16),
            pltpu.VMEM((rows, columns), BF16),
            pltpu.VMEM((2, 8, head_dim), F32),
            pltpu.VMEM((data, 8, head_dim), F32),
            pltpu.VMEM((chips, 8, head_dim), F32),
            dma((3,)),
            dma((3, chips)),
            dma((2, chips)),
            dma((2, chips, data)),
            dma((6,)),
            dma((2, chips, data)),
            dma((2, chips)),
            dma((2, data)),
            dma((2, data)),
            dma((2, chips)),
        ],
        compiler_params=pltpu.CompilerParams(
            collective_id=0, has_side_effects=True, vmem_limit_bytes=52 * 1024 * 1024
        ),
        cost_estimate=pl.CostEstimate(flops=2_000_000_000, bytes_accessed=6_000_000, transcendentals=300_000),
        name="kv_backward",
    )(
        hidden_row,
        queries[0],
        upstream[0],
        advantage,
        selected,
        segment,
        w_kv,
        k_gain.reshape(1, head_dim),
        q_gain.reshape(1, head_dim),
    )
    return (d_weight[:rows_dev], d_gain[0])


def solution(mesh):
    in_specs = (
        P(("dp", "fsdp"), None, None),
        P(("dp", "fsdp"), None, None),
        P(("dp", "fsdp"), None, None),
        P(("dp", "fsdp"), None),
        P(("dp", "fsdp"), None),
        P(("dp", "fsdp"), None),
        P("fsdp", None),
        P(),
        P(),
    )
    out_specs = (P("fsdp", None), P())
    return jax.shard_map(
        functools.partial(shards, mesh.shape["dp"], mesh.shape["fsdp"]),
        mesh=mesh,
        in_specs=in_specs,
        out_specs=out_specs,
        check_vma=False,
    )
```

```python
import functools
import math

import jax
import jax.numpy as jnp
from jax import lax
from jax.experimental import pallas as pl
from jax.experimental.pallas import tpu as pltpu
from jax.sharding import PartitionSpec as P

CAP = 128
epsilon = 1e-06
MESH = pl.DeviceIdType.MESH
F32 = jnp.float32
BF16 = jnp.bfloat16


def dot_last(a, b):
    return lax.dot_general(a, b, (((1,), (1,)), ((), ())), preferred_element_type=F32)


def dot(a, b):
    return jnp.dot(a, b, preferred_element_type=F32)


def body(
    grid,
    owners,
    hidden,
    queries,
    upstream,
    advantage,
    selected,
    segment,
    w_own,
    k_gain,
    q_gain,
    d_weight,
    d_gain,
    adv_in,
    sel_in,
    seg_in,
    kg_in,
    qg_in,
    hid,
    hid_t,
    w_half,
    q_raw,
    u_raw,
    q_sel,
    c_sel,
    allowed,
    kv_out,
    kv_own,
    kv_in,
    d_kv,
    part,
    mid_row,
    mid_col,
    relay_row,
    relay_col,
    from_row,
    from_col,
    z_out,
    from_z,
    final,
    gain_core,
    gain_data,
    gain_z,
    local_sem,
    hid_sem,
    w_z_sem,
    w_row_sem,
    w_col_sem,
    w_diag_row_sem,
    w_diag_col_sem,
    core_sem,
    mid_row_sem,
    mid_col_sem,
    row_sem,
    col_sem,
    z_sem,
    final_sem,
    gain_data_sem,
    gain_z_sem,
):
    tall, wide = grid
    data = tall * wide
    chips = owners // 2
    rows = w_own.shape[0]
    share = rows // data
    length = hidden.shape[0]
    head_dim = k_gain.shape[1]
    half = w_own.shape[1] // 2
    low, high = pl.ds(0, half), pl.ds(half, half)
    heads = queries.shape[1] // head_dim
    cap = allowed.shape[1] // 2
    scale = head_dim ** (-0.5)
    dp = lax.axis_index("dp")
    me = lax.axis_index("fsdp")
    chip = me // 2
    core = me % 2
    sibling = {"dp": dp, "fsdp": chip * 2 + 1 - core}

    def chip_at(k):
        return lax.rem(chip + k, chips)

    def data_at(k):
        return lax.rem(dp + k, data)

    row, col = dp // wide, dp % wide

    def place(s, t):
        return lax.rem(row + s, tall) * wide + lax.rem(col + t, wide)

    def to_chip(other):
        return {"dp": dp, "fsdp": other * 2 + core}

    def to_data(other):
        return {"dp": other, "fsdp": me}

    def rows_of(p):
        return pl.ds(pl.multiple_of(p * share, 16), share)

    def remote(src, dst, send, recv, device):
        return pltpu.make_async_remote_copy(
            src_ref=src, dst_ref=dst, send_sem=send, recv_sem=recv, device_id=device, device_id_type=MESH
        )

    own_w = pltpu.make_async_copy(w_own, w_half.at[chip], local_sem.at[0])
    own_w.start()
    load_q = pltpu.make_async_copy(queries, q_raw, local_sem.at[1])
    load_q.start()
    load_u = pltpu.make_async_copy(upstream, u_raw, local_sem.at[2])
    load_u.start()
    smalls = []
    for n, (src, dst) in enumerate(
        ((advantage, adv_in), (selected, sel_in), (segment, seg_in), (k_gain, kg_in), (q_gain, qg_in))
    ):
        load = pltpu.make_async_copy(src, dst, local_sem.at[3 + n])
        load.start()
        smalls.append(load)
    loads = []
    for j in range(chips):
        cols = pl.ds(pl.multiple_of((2 * j + core) * rows, 128), rows)
        load = pltpu.make_async_copy(
            hidden.at[:, cols], hid.at[0, :, pl.ds(j * rows, rows)], hid_sem.at[0, j]
        )
        load.start()
        loads.append(load)

    barrier = pltpu.get_barrier_semaphore()
    pl.semaphore_signal(barrier, inc=1, device_id=sibling, device_id_type=MESH)
    for k in range(1, chips):
        pl.semaphore_signal(barrier, inc=1, device_id=to_chip(chip_at(k)), device_id_type=MESH)
    for k in range(1, data):
        pl.semaphore_signal(barrier, inc=1, device_id=to_data(data_at(k)), device_id_type=MESH)
    pl.semaphore_wait(barrier, chips + data - 1)

    mine = rows_of(dp)
    sends = []
    for k in range(1, chips):
        copy = remote(
            w_own.at[mine], w_half.at[chip, mine], w_z_sem.at[0, k], w_z_sem.at[1, k], to_chip(chip_at(k))
        )
        copy.start()
        sends.append(copy)
    swaps = []
    for j in range(chips):
        cols = pl.ds(pl.multiple_of((2 * j + 1 - core) * rows, 128), rows)
        copy = remote(
            hidden.at[:, cols],
            hid.at[1, :, pl.ds(j * rows, rows)],
            hid_sem.at[1, j],
            hid_sem.at[2, j],
            sibling,
        )
        copy.start()
        swaps.append(copy)

    for load in smalls:
        load.wait()
    chosen = sel_in[...].astype(F32)
    places = lax.broadcasted_iota(jnp.int32, (length, length), 0)
    others = lax.broadcasted_iota(jnp.int32, (length, length), 1)
    upto = places <= others
    rank = dot(jnp.broadcast_to(chosen, (16, length)).astype(BF16), upto.astype(F32).astype(BF16))[:1]
    slots = lax.broadcasted_iota(jnp.int32, (cap, length), 0).astype(F32) + 1.0
    pick = jnp.where(rank == slots, chosen, 0.0)
    pick_b = pick.astype(BF16)
    token_weight = jnp.sum(pick * (adv_in[...] * chosen), axis=1, keepdims=True)
    groups = jnp.broadcast_to(seg_in[...].astype(F32), (length, length))
    allowed_full = jnp.where((groups == groups.T) & upto, 1.0, 0.0).astype(BF16)
    allowed_sel = dot_last(allowed_full, pick_b)
    allowed[:, :cap] = allowed_sel
    allowed[:, cap:] = allowed_sel

    ahead = []
    near = {}
    diag = {}

    def forward(k):
        sends[k - 1].wait_recv()
        source = chip_at(chips - k)
        for t in range(1, wide):
            near[k, 0, t] = remote(
                w_half.at[source, mine],
                w_half.at[source, mine],
                w_row_sem.at[0, k, t - 1],
                w_row_sem.at[1, k, t - 1],
                to_data(place(0, t)),
            )
        for s in range(1, tall):
            near[k, s, 0] = remote(
                w_half.at[source, mine],
                w_half.at[source, mine],
                w_col_sem.at[0, k, s - 1],
                w_col_sem.at[1, k, s - 1],
                to_data(place(s, 0)),
            )
        for copy in [near[key] for key in near if key[0] == k]:
            copy.start()
            ahead.append(copy)

    def forward_diag(k):
        source = chip_at(chips - k)
        for t in range(1, wide):
            near[k, 0, t].wait_recv()
            block = w_half.at[source, rows_of(place(0, wide - t)), low]
            for s in range(1, tall):
                diag[k, 0, s, t] = remote(
                    block, block, w_diag_row_sem.at[0, k, s - 1, t - 1], w_diag_row_sem.at[1, k, s - 1, t - 1], to_data(place(s, 0))
                )
                diag[k, 0, s, t].start()
                ahead.append(diag[k, 0, s, t])
        for s in range(1, tall):
            near[k, s, 0].wait_recv()
            block = w_half.at[source, rows_of(place(tall - s, 0)), high]
            for t in range(1, wide):
                diag[k, 1, s, t] = remote(
                    block, block, w_diag_col_sem.at[0, k, s - 1, t - 1], w_diag_col_sem.at[1, k, s - 1, t - 1], to_data(place(0, t))
                )
                diag[k, 1, s, t].start()
                ahead.append(diag[k, 1, s, t])

    for k in range(1, chips):
        forward(k)
        if k > 1:
            forward_diag(k - 1)

    load_q.wait()
    load_u.wait()
    for h in range(heads):
        lanes = pl.ds(h * head_dim, head_dim)
        query = dot(pick_b, q_raw[:, lanes])
        query_scale = lax.rsqrt(jnp.mean(query * query, axis=-1, keepdims=True) + epsilon)
        q_sel[pl.ds(h * cap, cap)] = (query * query_scale * qg_in[...]).astype(BF16)
        grad = dot(pick_b, u_raw[:, lanes])
        c_sel[pl.ds(h * cap, cap)] = (token_weight * grad).astype(BF16)

    if chips > 1:
        forward_diag(chips - 1)
    for j in range(chips):
        loads[j].wait()
        hid_t[pl.ds(j * rows, rows), :length] = hid[0, :, pl.ds(j * rows, rows)].T
    for j in range(chips):
        swaps[j].wait()
        hid_t[pl.ds(j * rows, rows), length:] = hid[1, :, pl.ds(j * rows, rows)].T

    own_w.wait()
    for k in range(chips):
        source = chip_at(chips - k)
        for key in diag:
            if key[0] == k:
                diag[key].wait_recv()
        cols = pl.ds(pl.multiple_of(source * rows, 128), rows)
        weight = w_half[source]
        if k == 0:
            kv_out[...] = dot(hid[1, :, cols], weight)
            kv_own[...] = dot(hid[0, :, cols], weight)
        elif k < chips - 1:
            kv_out[...] += dot(hid[1, :, cols], weight)
            kv_own[...] += dot(hid[0, :, cols], weight)
        else:
            kv_out[...] += dot(hid[1, :, cols], weight)
    swap_kv = remote(kv_out, kv_in, core_sem.at[0], core_sem.at[1], sibling)
    swap_kv.start()
    key_value = kv_own[...]
    if chips > 1:
        key_value += dot(hid[0, :, cols], weight)
    swap_kv.wait()
    key_value = key_value + kv_in[...]

    k_raw = key_value[:, :head_dim]
    k_scale = lax.rsqrt(jnp.mean(k_raw * k_raw, axis=-1, keepdims=True) + epsilon)
    k_hat = k_raw * k_scale
    k_norm = (k_hat * kg_in[...]).astype(BF16)
    values = key_value[:, head_dim:].astype(BF16)
    d_key = jnp.zeros((length, head_dim), F32)
    d_value = jnp.zeros((length, head_dim), F32)
    for h in range(heads // 2):
        pair = pl.ds(h * 2 * cap, 2 * cap)
        q_pair = q_sel[pair]
        c_pair = c_sel[pair]
        expo = jnp.exp(dot_last(k_norm, q_pair) * scale) * allowed[...]
        total = jnp.sum(expo, axis=0, keepdims=True)
        probs = expo * (1.0 / jnp.where(total > 0.0, total, 1.0))
        probs_b = probs.astype(BF16)
        dprob = dot_last(values, c_pair)
        delta = jnp.sum(probs_b.astype(F32) * dprob, axis=0, keepdims=True)
        dscore = (probs * (dprob - delta) * scale).astype(BF16)
        d_key += dot(dscore, q_pair)
        d_value += dot(probs_b, c_pair)
    d_khat = d_key * kg_in[...]
    d_kraw = k_scale * (d_khat - k_hat * jnp.mean(d_khat * k_hat, axis=-1, keepdims=True))
    d_kv[0, :, :head_dim] = d_kraw.astype(BF16)
    d_kv[0, :, head_dim:] = d_value.astype(BF16)
    swap_d = remote(d_kv.at[0], d_kv.at[1], core_sem.at[2], core_sem.at[3], sibling)
    swap_d.start()
    gain = jnp.sum(d_key * k_hat, axis=0, keepdims=True)
    gain_core[0] = jnp.broadcast_to(gain, (8, head_dim))
    swap_g = remote(gain_core.at[0], gain_core.at[1], core_sem.at[4], core_sem.at[5], sibling)
    swap_g.start()
    parts = []
    mids = {}
    nears = {}
    columns = []
    gains = []

    def begin(copy):
        copy.start()
        parts.append(copy)
        return copy

    def make(k):
        target = chip_at(k)
        block = pl.ds(pl.multiple_of(target * rows, 128), rows)
        if k == 1:
            mixed = dot(hid_t[block, :length], d_kv[0])
            swap_d.wait()
            part[target] = (mixed + dot(hid_t[block, length:], d_kv[1])).astype(BF16)
        else:
            part[target] = dot(hid_t[block, :], d_kv[...].reshape(2 * length, 2 * half)).astype(BF16)
        for s in range(1, tall):
            for t in range(1, wide):
                share_of = rows_of(place(s, t))
                mids[k, 0, s, t] = begin(
                    remote(
                        part.at[target, share_of, low],
                        mid_row.at[k - 1, s, t],
                        mid_row_sem.at[0, k - 1, s - 1, t - 1],
                        mid_row_sem.at[1, k - 1, s - 1, t - 1],
                        to_data(place(0, t)),
                    )
                )
                mids[k, 1, s, t] = begin(
                    remote(
                        part.at[target, share_of, high],
                        mid_col.at[k - 1, s, t],
                        mid_col_sem.at[0, k - 1, s - 1, t - 1],
                        mid_col_sem.at[1, k - 1, s - 1, t - 1],
                        to_data(place(s, 0)),
                    )
                )
        for t in range(1, wide):
            nears[k, 0, t, 0] = begin(
                remote(
                    part.at[target, rows_of(place(0, t)), low],
                    from_row.at[t, k - 1, :, low],
                    row_sem.at[0, 0, k - 1, t - 1],
                    row_sem.at[1, 0, k - 1, t - 1],
                    to_data(place(0, t)),
                )
            )
        for s in range(1, tall):
            nears[k, s, 0, 1] = begin(
                remote(
                    part.at[target, rows_of(place(s, 0)), high],
                    from_col.at[s, k - 1, :, high],
                    col_sem.at[0, 0, k - 1, s - 1],
                    col_sem.at[1, 0, k - 1, s - 1],
                    to_data(place(s, 0)),
                )
            )

    def relay(k):
        target = chip_at(k)
        for s in range(1, tall):
            sent = part[target, rows_of(place(s, 0)), low].astype(F32)
            for t in range(1, wide):
                mids[k, 0, s, t].wait_recv()
                sent += mid_row[k - 1, s, t].astype(F32)
            relay_col[k - 1, s] = sent.astype(BF16)
            nears[k, s, 0, 0] = begin(
                remote(
                    relay_col.at[k - 1, s],
                    from_col.at[s, k - 1, :, low],
                    col_sem.at[0, 1, k - 1, s - 1],
                    col_sem.at[1, 1, k - 1, s - 1],
                    to_data(place(s, 0)),
                )
            )
        for t in range(1, wide):
            sent = part[target, rows_of(place(0, t)), high].astype(F32)
            for s in range(1, tall):
                mids[k, 1, s, t].wait_recv()
                sent += mid_col[k - 1, s, t].astype(F32)
            relay_row[k - 1, t] = sent.astype(BF16)
            nears[k, 0, t, 1] = begin(
                remote(
                    relay_row.at[k - 1, t],
                    from_row.at[t, k - 1, :, high],
                    row_sem.at[0, 1, k - 1, t - 1],
                    row_sem.at[1, 1, k - 1, t - 1],
                    to_data(place(0, t)),
                )
            )

    def collect(k):
        target = chip_at(k)
        for key in nears:
            if key[0] == k:
                nears[key].wait_recv()
        total = part[target, mine].astype(F32)
        for s in range(1, tall):
            total += from_col[s, k - 1].astype(F32)
        for t in range(1, wide):
            total += from_row[t, k - 1].astype(F32)
        if k < chips:
            z_out[k] = total.astype(BF16)
            copy = remote(z_out.at[k], from_z.at[k], z_sem.at[0, k], z_sem.at[1, k], to_chip(target))
            copy.start()
            columns.append(copy)
        return total

    for k in range(1, chips + 3):
        if k <= chips:
            make(k)
        if k == 1:
            swap_g.wait()
            gain_data[dp] = gain_core[0] + gain_core[1]
            for d in range(1, data):
                copy = remote(
                    gain_data.at[dp], gain_data.at[dp], gain_data_sem.at[0, d], gain_data_sem.at[1, d], to_data(data_at(d))
                )
                copy.start()
                gains.append(copy)
        if 1 <= k - 1 <= chips:
            relay(k - 1)
        if 1 <= k - 2 <= chips:
            summed = collect(k - 2)

    for copy in gains:
        copy.wait()
    gain_sum = gain_data[0]
    for d in range(1, data):
        gain_sum += gain_data[d]
    gain_z[chip] = gain_sum
    z_gains = []
    for k in range(1, chips):
        copy = remote(
            gain_z.at[chip], gain_z.at[chip], gain_z_sem.at[0, k], gain_z_sem.at[1, k], to_chip(chip_at(k))
        )
        copy.start()
        z_gains.append(copy)

    for k in range(1, chips):
        columns[k - 1].wait_recv()
        summed += from_z[k].astype(F32)
    final[mine] = summed.astype(BF16)
    finals = []
    for d in range(1, data):
        copy = remote(final.at[mine], final.at[mine], final_sem.at[0, d], final_sem.at[1, d], to_data(data_at(d)))
        copy.start()
        finals.append(copy)

    for copy in z_gains:
        copy.wait()
    gain_sum = gain_z[0]
    for k in range(1, chips):
        gain_sum += gain_z[k]
    d_gain[...] = gain_sum

    for copy in sends + ahead + parts + columns:
        copy.wait_send()
    for copy in finals:
        copy.wait()
    d_weight[...] = final[...]


def shards(grid, owners, hidden, queries, upstream, advantage, selected, segment, w_kv, k_gain, q_gain):
    hidden_row = hidden[0]
    length, width = hidden_row.shape
    rows_dev, columns = w_kv.shape
    head_dim = k_gain.shape[0]
    heads = queries.shape[2] // head_dim
    tall, wide = grid
    data = tall * wide
    unit = math.lcm(128, 16 * data)
    rows = -(-rows_dev // unit) * unit
    chips = owners // 2
    share = rows // data
    if rows_dev * owners != width:
        hidden_row = jnp.pad(hidden_row, ((0, 0), (0, rows_dev * owners - width)))
    if rows != rows_dev:
        blocks = hidden_row.reshape(length, owners, rows_dev)
        hidden_row = jnp.pad(blocks, ((0, 0), (0, 0), (0, rows - rows_dev))).reshape(length, owners * rows)
        w_kv = jnp.pad(w_kv, ((0, rows - rows_dev), (0, 0)))
    vmem = pl.BlockSpec(memory_space=pltpu.VMEM)
    hbm = pl.BlockSpec(memory_space=pltpu.HBM)
    dma = pltpu.SemaphoreType.DMA
    d_weight, d_gain = pl.pallas_call(
        functools.partial(body, grid, owners),
        out_shape=(
            jax.ShapeDtypeStruct((rows, columns), BF16),
            jax.ShapeDtypeStruct((8, head_dim), F32),
        ),
        in_specs=[hbm] * 9,
        out_specs=(vmem, vmem),
        scratch_shapes=[
            pltpu.VMEM((1, length), F32),
            pltpu.VMEM((1, length), jnp.int32),
            pltpu.VMEM((1, length), jnp.int32),
            pltpu.VMEM((1, head_dim), F32),
            pltpu.VMEM((1, head_dim), F32),
            pltpu.VMEM((2, length, chips * rows), BF16),
            pltpu.VMEM((chips * rows, 2 * length), BF16),
            pltpu.VMEM((chips, rows, columns), BF16),
            pltpu.VMEM((length, heads * head_dim), BF16),
            pltpu.VMEM((length, heads * head_dim), BF16),
            pltpu.VMEM((heads * CAP, head_dim), BF16),
            pltpu.VMEM((heads * CAP, head_dim), BF16),
            pltpu.VMEM((length, 2 * CAP), F32),
            pltpu.VMEM((length, columns), F32),
            pltpu.VMEM((length, columns), F32),
            pltpu.VMEM((length, columns), F32),
            pltpu.VMEM((2, length, columns), BF16),
            pltpu.VMEM((chips, rows, columns), BF16),
            pltpu.VMEM((chips, tall, wide, share, columns // 2), BF16),
            pltpu.VMEM((chips, tall, wide, share, columns // 2), BF16),
            pltpu.VMEM((chips, wide, share, columns // 2), BF16),
            pltpu.VMEM((chips, tall, share, columns // 2), BF16),
            pltpu.VMEM((wide, chips, share, columns), BF16),
            pltpu.VMEM((tall, chips, share, columns), BF16),
            pltpu.VMEM((chips, share, columns), BF16),
            pltpu.VMEM((chips, share, columns), BF16),
            pltpu.VMEM((rows, columns), BF16),
            pltpu.VMEM((2, 8, head_dim), F32),
            pltpu.VMEM((data, 8, head_dim), F32),
            pltpu.VMEM((chips, 8, head_dim), F32),
            dma((8,)),
            dma((3, chips)),
            dma((2, chips)),
            dma((2, chips, max(wide - 1, 1))),
            dma((2, chips, max(tall - 1, 1))),
            dma((2, chips, max(tall - 1, 1), max(wide - 1, 1))),
            dma((2, chips, max(tall - 1, 1), max(wide - 1, 1))),
            dma((6,)),
            dma((2, chips, max(tall - 1, 1), max(wide - 1, 1))),
            dma((2, chips, max(tall - 1, 1), max(wide - 1, 1))),
            dma((2, 2, chips, max(wide - 1, 1))),
            dma((2, 2, chips, max(tall - 1, 1))),
            dma((2, chips)),
            dma((2, data)),
            dma((2, data)),
            dma((2, chips)),
        ],
        compiler_params=pltpu.CompilerParams(
            collective_id=0, has_side_effects=True, vmem_limit_bytes=64 * 1024 * 1024
        ),
        cost_estimate=pl.CostEstimate(flops=2_000_000_000, bytes_accessed=6_000_000, transcendentals=300_000),
        name="kv_backward",
    )(
        hidden_row,
        queries[0],
        upstream[0],
        advantage,
        selected,
        segment,
        w_kv,
        k_gain.reshape(1, head_dim),
        q_gain.reshape(1, head_dim),
    )
    return (d_weight[:rows_dev].astype(F32), d_gain[0])


def solution(mesh):
    in_specs = (
        P(("dp", "fsdp"), None, None),
        P(("dp", "fsdp"), None, None),
        P(("dp", "fsdp"), None, None),
        P(("dp", "fsdp"), None),
        P(("dp", "fsdp"), None),
        P(("dp", "fsdp"), None),
        P("fsdp", None),
        P(),
        P(),
    )
    out_specs = (P("fsdp", None), P())
    data = mesh.shape["dp"]
    tall = max(n for n in range(1, math.isqrt(data) + 1) if data % n == 0)
    return jax.shard_map(
        functools.partial(shards, (tall, data // tall), mesh.shape["fsdp"]),
        mesh=mesh,
        in_specs=in_specs,
        out_specs=out_specs,
        check_vma=False,
    )
```

```python
import functools
import math

import jax
import jax.numpy as jnp
from jax import lax
from jax.experimental import pallas as pl
from jax.experimental.pallas import tpu as pltpu
from jax.sharding import PartitionSpec as P

CAP = 128
epsilon = 1e-06
MESH = pl.DeviceIdType.MESH
F32 = jnp.float32
BF16 = jnp.bfloat16


def dot_last(a, b):
    return lax.dot_general(a, b, (((1,), (1,)), ((), ())), preferred_element_type=F32)


def dot(a, b):
    return jnp.dot(a, b, preferred_element_type=F32)


def body(
    grid,
    owners,
    hidden,
    queries,
    upstream,
    advantage,
    selected,
    segment,
    w_own,
    k_gain,
    q_gain,
    d_weight,
    d_gain,
    adv_in,
    sel_in,
    seg_in,
    kg_in,
    qg_in,
    hid,
    hid_t,
    w_half,
    q_raw,
    u_raw,
    q_sel,
    c_sel,
    q_sel_t,
    c_sel_t,
    probs_all,
    dscore_all,
    allowed,
    kv_out,
    kv_own,
    kv_in,
    d_kv,
    part,
    mid_row,
    mid_col,
    relay_row,
    relay_col,
    from_row,
    from_col,
    z_out,
    from_z,
    final,
    gain_core,
    gain_data,
    gain_z,
    local_sem,
    hid_sem,
    w_z_sem,
    w_row_sem,
    w_col_sem,
    w_diag_row_sem,
    w_diag_col_sem,
    core_sem,
    mid_row_sem,
    mid_col_sem,
    row_sem,
    col_sem,
    z_sem,
    final_sem,
    gain_data_sem,
    gain_z_sem,
):
    tall, wide = grid
    data = tall * wide
    chips = owners // 2
    rows = w_own.shape[0]
    share = rows // data
    length = hidden.shape[0]
    head_dim = k_gain.shape[1]
    half = w_own.shape[1] // 2
    low, high = pl.ds(0, half), pl.ds(half, half)
    heads = queries.shape[1] // head_dim
    cap = allowed.shape[1] // 2
    scale = head_dim ** (-0.5)
    dp = lax.axis_index("dp")
    me = lax.axis_index("fsdp")
    chip = me // 2
    core = me % 2
    sibling = {"dp": dp, "fsdp": chip * 2 + 1 - core}

    def chip_at(k):
        return lax.rem(chip + k, chips)

    def data_at(k):
        return lax.rem(dp + k, data)

    row, col = dp // wide, dp % wide

    def place(s, t):
        return lax.rem(row + s, tall) * wide + lax.rem(col + t, wide)

    def to_chip(other):
        return {"dp": dp, "fsdp": other * 2 + core}

    def to_data(other):
        return {"dp": other, "fsdp": me}

    def rows_of(p):
        return pl.ds(pl.multiple_of(p * share, 16), share)

    def remote(src, dst, send, recv, device):
        return pltpu.make_async_remote_copy(
            src_ref=src, dst_ref=dst, send_sem=send, recv_sem=recv, device_id=device, device_id_type=MESH
        )

    own_w = pltpu.make_async_copy(w_own, w_half.at[chip], local_sem.at[0])
    own_w.start()
    load_q = pltpu.make_async_copy(queries, q_raw, local_sem.at[1])
    load_q.start()
    load_u = pltpu.make_async_copy(upstream, u_raw, local_sem.at[2])
    load_u.start()
    smalls = []
    for n, (src, dst) in enumerate(
        ((advantage, adv_in), (selected, sel_in), (segment, seg_in), (k_gain, kg_in), (q_gain, qg_in))
    ):
        load = pltpu.make_async_copy(src, dst, local_sem.at[3 + n])
        load.start()
        smalls.append(load)
    loads = []
    for j in range(chips):
        cols = pl.ds(pl.multiple_of((2 * j + core) * rows, 128), rows)
        load = pltpu.make_async_copy(
            hidden.at[:, cols], hid.at[0, :, pl.ds(j * rows, rows)], hid_sem.at[0, j]
        )
        load.start()
        loads.append(load)

    barrier = pltpu.get_barrier_semaphore()
    pl.semaphore_signal(barrier, inc=1, device_id=sibling, device_id_type=MESH)
    for k in range(1, chips):
        pl.semaphore_signal(barrier, inc=1, device_id=to_chip(chip_at(k)), device_id_type=MESH)
    for k in range(1, data):
        pl.semaphore_signal(barrier, inc=1, device_id=to_data(data_at(k)), device_id_type=MESH)
    pl.semaphore_wait(barrier, chips + data - 1)

    mine = rows_of(dp)
    sends = []
    for k in range(1, chips):
        copy = remote(
            w_own.at[mine], w_half.at[chip, mine], w_z_sem.at[0, k], w_z_sem.at[1, k], to_chip(chip_at(k))
        )
        copy.start()
        sends.append(copy)
    swaps = []
    for j in range(chips):
        cols = pl.ds(pl.multiple_of((2 * j + 1 - core) * rows, 128), rows)
        copy = remote(
            hidden.at[:, cols],
            hid.at[1, :, pl.ds(j * rows, rows)],
            hid_sem.at[1, j],
            hid_sem.at[2, j],
            sibling,
        )
        copy.start()
        swaps.append(copy)

    for load in smalls:
        load.wait()
    chosen = sel_in[...].astype(F32)
    places = lax.broadcasted_iota(jnp.int32, (length, length), 0)
    others = lax.broadcasted_iota(jnp.int32, (length, length), 1)
    upto = places <= others
    rank = dot(jnp.broadcast_to(chosen, (16, length)).astype(BF16), upto.astype(F32).astype(BF16))[:1]
    slots = lax.broadcasted_iota(jnp.int32, (cap, length), 0).astype(F32) + 1.0
    pick = jnp.where(rank == slots, chosen, 0.0)
    pick_b = pick.astype(BF16)
    token_weight = jnp.sum(pick * (adv_in[...] * chosen), axis=1, keepdims=True)
    groups = jnp.broadcast_to(seg_in[...].astype(F32), (length, length))
    allowed_full = jnp.where((groups == groups.T) & upto, 1.0, 0.0).astype(BF16)
    allowed_sel = dot_last(allowed_full, pick_b)
    allowed[:, :cap] = allowed_sel
    allowed[:, cap:] = allowed_sel

    ahead = []
    near = {}
    diag = {}

    def forward(k):
        sends[k - 1].wait_recv()
        source = chip_at(chips - k)
        for t in range(1, wide):
            near[k, 0, t] = remote(
                w_half.at[source, mine],
                w_half.at[source, mine],
                w_row_sem.at[0, k, t - 1],
                w_row_sem.at[1, k, t - 1],
                to_data(place(0, t)),
            )
        for s in range(1, tall):
            near[k, s, 0] = remote(
                w_half.at[source, mine],
                w_half.at[source, mine],
                w_col_sem.at[0, k, s - 1],
                w_col_sem.at[1, k, s - 1],
                to_data(place(s, 0)),
            )
        for copy in [near[key] for key in near if key[0] == k]:
            copy.start()
            ahead.append(copy)

    def forward_diag(k):
        source = chip_at(chips - k)
        for t in range(1, wide):
            near[k, 0, t].wait_recv()
            block = w_half.at[source, rows_of(place(0, wide - t)), low]
            for s in range(1, tall):
                diag[k, 0, s, t] = remote(
                    block, block, w_diag_row_sem.at[0, k, s - 1, t - 1], w_diag_row_sem.at[1, k, s - 1, t - 1], to_data(place(s, 0))
                )
                diag[k, 0, s, t].start()
                ahead.append(diag[k, 0, s, t])
        for s in range(1, tall):
            near[k, s, 0].wait_recv()
            block = w_half.at[source, rows_of(place(tall - s, 0)), high]
            for t in range(1, wide):
                diag[k, 1, s, t] = remote(
                    block, block, w_diag_col_sem.at[0, k, s - 1, t - 1], w_diag_col_sem.at[1, k, s - 1, t - 1], to_data(place(0, t))
                )
                diag[k, 1, s, t].start()
                ahead.append(diag[k, 1, s, t])

    def prepare_head(h):
        lanes = pl.ds(h * head_dim, head_dim)
        rows_h = pl.ds(h * cap, cap)
        query = dot(pick_b, q_raw[:, lanes])
        query_scale = lax.rsqrt(jnp.mean(query * query, axis=-1, keepdims=True) + epsilon)
        query = query * query_scale * qg_in[...]
        q_sel[rows_h] = query.astype(BF16)
        q_sel_t[:, rows_h] = query.T.astype(BF16)
        grad = token_weight * dot(pick_b, u_raw[:, lanes])
        c_sel[rows_h] = grad.astype(BF16)
        c_sel_t[:, rows_h] = grad.T.astype(BF16)

    def turn_own(j):
        loads[j].wait()
        hid_t[pl.ds(j * rows, rows), :length] = hid[0, :, pl.ds(j * rows, rows)].T

    def turn_swapped(j):
        swaps[j].wait()
        hid_t[pl.ds(j * rows, rows), length:] = hid[1, :, pl.ds(j * rows, rows)].T

    tasks = [functools.partial(prepare_head, h) for h in range(heads)]
    tasks += [functools.partial(turn_own, j) for j in range(chips)]
    tasks += [functools.partial(turn_swapped, j) for j in range(chips)]
    events = []
    for k in range(1, chips):
        events.append(functools.partial(forward, k))
        if k > 1:
            events.append(functools.partial(forward_diag, k - 1))
    if chips > 1:
        events.append(functools.partial(forward_diag, chips - 1))
    load_q.wait()
    load_u.wait()
    done = 0
    for n, event in enumerate(events):
        until = len(tasks) * (n + 1) // (len(events) + 1)
        for task in tasks[done:until]:
            task()
        done = until
        event()
    for task in tasks[done:]:
        task()

    own_w.wait()
    for k in range(chips):
        source = chip_at(chips - k)
        for key in diag:
            if key[0] == k:
                diag[key].wait_recv()
        cols = pl.ds(pl.multiple_of(source * rows, 128), rows)
        weight = w_half[source]
        if k == 0:
            kv_out[...] = dot(hid[1, :, cols], weight)
            kv_own[...] = dot(hid[0, :, cols], weight)
        elif k < chips - 1:
            kv_out[...] += dot(hid[1, :, cols], weight)
            kv_own[...] += dot(hid[0, :, cols], weight)
        else:
            kv_out[...] += dot(hid[1, :, cols], weight)
    swap_kv = remote(kv_out, kv_in, core_sem.at[0], core_sem.at[1], sibling)
    swap_kv.start()
    key_value = kv_own[...]
    if chips > 1:
        key_value += dot(hid[0, :, cols], weight)
    swap_kv.wait()
    key_value = key_value + kv_in[...]

    k_raw = key_value[:, :head_dim]
    k_scale = lax.rsqrt(jnp.mean(k_raw * k_raw, axis=-1, keepdims=True) + epsilon)
    k_hat = k_raw * k_scale
    k_norm = (k_hat * kg_in[...]).astype(BF16)
    values = key_value[:, head_dim:].astype(BF16)
    for h in range(heads // 2):
        pair = pl.ds(h * 2 * cap, 2 * cap)
        expo = jnp.exp(dot(k_norm, q_sel_t[:, pair]) * scale) * allowed[...]
        total = jnp.sum(expo, axis=0, keepdims=True)
        probs = expo * (1.0 / jnp.where(total > 0.0, total, 1.0))
        probs_b = probs.astype(BF16)
        probs_all[:, pair] = probs_b
        dprob = dot(values, c_sel_t[:, pair])
        delta = jnp.sum(probs_b.astype(F32) * dprob, axis=0, keepdims=True)
        dscore_all[:, pair] = (probs * (dprob - delta) * scale).astype(BF16)
    d_key = dot(dscore_all[...], q_sel[...])
    d_value = dot(probs_all[...], c_sel[...])
    d_khat = d_key * kg_in[...]
    d_kraw = k_scale * (d_khat - k_hat * jnp.mean(d_khat * k_hat, axis=-1, keepdims=True))
    d_kv[0, :, :head_dim] = d_kraw.astype(BF16)
    d_kv[0, :, head_dim:] = d_value.astype(BF16)
    swap_d = remote(d_kv.at[0], d_kv.at[1], core_sem.at[2], core_sem.at[3], sibling)
    swap_d.start()
    gain = jnp.sum(d_key * k_hat, axis=0, keepdims=True)
    gain_core[0] = jnp.broadcast_to(gain, (8, head_dim))
    swap_g = remote(gain_core.at[0], gain_core.at[1], core_sem.at[4], core_sem.at[5], sibling)
    swap_g.start()
    parts = []
    mids = {}
    nears = {}
    columns = []
    gains = []

    def begin(copy):
        copy.start()
        parts.append(copy)
        return copy

    def make(k):
        target = chip_at(k)
        block = pl.ds(pl.multiple_of(target * rows, 128), rows)
        if k == 1:
            mixed = dot(hid_t[block, :length], d_kv[0])
            swap_d.wait()
            part[target] = (mixed + dot(hid_t[block, length:], d_kv[1])).astype(BF16)
        else:
            part[target] = dot(hid_t[block, :], d_kv[...].reshape(2 * length, 2 * half)).astype(BF16)
        for s in range(1, tall):
            for t in range(1, wide):
                share_of = rows_of(place(s, t))
                mids[k, 0, s, t] = begin(
                    remote(
                        part.at[target, share_of, low],
                        mid_row.at[k - 1, s, t],
                        mid_row_sem.at[0, k - 1, s - 1, t - 1],
                        mid_row_sem.at[1, k - 1, s - 1, t - 1],
                        to_data(place(0, t)),
                    )
                )
                mids[k, 1, s, t] = begin(
                    remote(
                        part.at[target, share_of, high],
                        mid_col.at[k - 1, s, t],
                        mid_col_sem.at[0, k - 1, s - 1, t - 1],
                        mid_col_sem.at[1, k - 1, s - 1, t - 1],
                        to_data(place(s, 0)),
                    )
                )
        for t in range(1, wide):
            nears[k, 0, t, 0] = begin(
                remote(
                    part.at[target, rows_of(place(0, t)), low],
                    from_row.at[t, k - 1, :, low],
                    row_sem.at[0, 0, k - 1, t - 1],
                    row_sem.at[1, 0, k - 1, t - 1],
                    to_data(place(0, t)),
                )
            )
        for s in range(1, tall):
            nears[k, s, 0, 1] = begin(
                remote(
                    part.at[target, rows_of(place(s, 0)), high],
                    from_col.at[s, k - 1, :, high],
                    col_sem.at[0, 0, k - 1, s - 1],
                    col_sem.at[1, 0, k - 1, s - 1],
                    to_data(place(s, 0)),
                )
            )

    def relay(k):
        target = chip_at(k)
        for s in range(1, tall):
            sent = part[target, rows_of(place(s, 0)), low].astype(F32)
            for t in range(1, wide):
                mids[k, 0, s, t].wait_recv()
                sent += mid_row[k - 1, s, t].astype(F32)
            relay_col[k - 1, s] = sent.astype(BF16)
            nears[k, s, 0, 0] = begin(
                remote(
                    relay_col.at[k - 1, s],
                    from_col.at[s, k - 1, :, low],
                    col_sem.at[0, 1, k - 1, s - 1],
                    col_sem.at[1, 1, k - 1, s - 1],
                    to_data(place(s, 0)),
                )
            )
        for t in range(1, wide):
            sent = part[target, rows_of(place(0, t)), high].astype(F32)
            for s in range(1, tall):
                mids[k, 1, s, t].wait_recv()
                sent += mid_col[k - 1, s, t].astype(F32)
            relay_row[k - 1, t] = sent.astype(BF16)
            nears[k, 0, t, 1] = begin(
                remote(
                    relay_row.at[k - 1, t],
                    from_row.at[t, k - 1, :, high],
                    row_sem.at[0, 1, k - 1, t - 1],
                    row_sem.at[1, 1, k - 1, t - 1],
                    to_data(place(0, t)),
                )
            )

    def collect(k):
        target = chip_at(k)
        for key in nears:
            if key[0] == k:
                nears[key].wait_recv()
        total = part[target, mine].astype(F32)
        for s in range(1, tall):
            total += from_col[s, k - 1].astype(F32)
        for t in range(1, wide):
            total += from_row[t, k - 1].astype(F32)
        if k < chips:
            z_out[k] = total.astype(BF16)
            copy = remote(z_out.at[k], from_z.at[k], z_sem.at[0, k], z_sem.at[1, k], to_chip(target))
            copy.start()
            columns.append(copy)
        return total

    for k in range(1, chips + 3):
        if k <= chips:
            make(k)
        if k == 1:
            swap_g.wait()
            gain_data[dp] = gain_core[0] + gain_core[1]
            for d in range(1, data):
                copy = remote(
                    gain_data.at[dp], gain_data.at[dp], gain_data_sem.at[0, d], gain_data_sem.at[1, d], to_data(data_at(d))
                )
                copy.start()
                gains.append(copy)
        if 1 <= k - 1 <= chips:
            relay(k - 1)
        if 1 <= k - 2 <= chips:
            summed = collect(k - 2)

    for copy in gains:
        copy.wait()
    gain_sum = gain_data[0]
    for d in range(1, data):
        gain_sum += gain_data[d]
    gain_z[chip] = gain_sum
    z_gains = []
    for k in range(1, chips):
        copy = remote(
            gain_z.at[chip], gain_z.at[chip], gain_z_sem.at[0, k], gain_z_sem.at[1, k], to_chip(chip_at(k))
        )
        copy.start()
        z_gains.append(copy)

    for k in range(1, chips):
        columns[k - 1].wait_recv()
        summed += from_z[k].astype(F32)
    final[mine] = summed.astype(BF16)
    finals = []
    for d in range(1, data):
        copy = remote(final.at[mine], final.at[mine], final_sem.at[0, d], final_sem.at[1, d], to_data(data_at(d)))
        copy.start()
        finals.append(copy)

    for copy in z_gains:
        copy.wait()
    gain_sum = gain_z[0]
    for k in range(1, chips):
        gain_sum += gain_z[k]
    d_gain[...] = gain_sum

    for copy in sends + ahead + parts + columns:
        copy.wait_send()
    for copy in finals:
        copy.wait()
    d_weight[...] = final[...]


def shards(grid, owners, hidden, queries, upstream, advantage, selected, segment, w_kv, k_gain, q_gain):
    hidden_row = hidden[0]
    length, width = hidden_row.shape
    rows_dev, columns = w_kv.shape
    head_dim = k_gain.shape[0]
    heads = queries.shape[2] // head_dim
    tall, wide = grid
    data = tall * wide
    unit = math.lcm(128, 16 * data)
    rows = -(-rows_dev // unit) * unit
    chips = owners // 2
    share = rows // data
    if rows_dev * owners != width:
        hidden_row = jnp.pad(hidden_row, ((0, 0), (0, rows_dev * owners - width)))
    if rows != rows_dev:
        blocks = hidden_row.reshape(length, owners, rows_dev)
        hidden_row = jnp.pad(blocks, ((0, 0), (0, 0), (0, rows - rows_dev))).reshape(length, owners * rows)
        w_kv = jnp.pad(w_kv, ((0, rows - rows_dev), (0, 0)))
    vmem = pl.BlockSpec(memory_space=pltpu.VMEM)
    hbm = pl.BlockSpec(memory_space=pltpu.HBM)
    dma = pltpu.SemaphoreType.DMA
    d_weight, d_gain = pl.pallas_call(
        functools.partial(body, grid, owners),
        out_shape=(
            jax.ShapeDtypeStruct((rows, columns), BF16),
            jax.ShapeDtypeStruct((8, head_dim), F32),
        ),
        in_specs=[hbm] * 9,
        out_specs=(vmem, vmem),
        scratch_shapes=[
            pltpu.VMEM((1, length), F32),
            pltpu.VMEM((1, length), jnp.int32),
            pltpu.VMEM((1, length), jnp.int32),
            pltpu.VMEM((1, head_dim), F32),
            pltpu.VMEM((1, head_dim), F32),
            pltpu.VMEM((2, length, chips * rows), BF16),
            pltpu.VMEM((chips * rows, 2 * length), BF16),
            pltpu.VMEM((chips, rows, columns), BF16),
            pltpu.VMEM((length, heads * head_dim), BF16),
            pltpu.VMEM((length, heads * head_dim), BF16),
            pltpu.VMEM((heads * CAP, head_dim), BF16),
            pltpu.VMEM((heads * CAP, head_dim), BF16),
            pltpu.VMEM((head_dim, heads * CAP), BF16),
            pltpu.VMEM((head_dim, heads * CAP), BF16),
            pltpu.VMEM((length, heads * CAP), BF16),
            pltpu.VMEM((length, heads * CAP), BF16),
            pltpu.VMEM((length, 2 * CAP), F32),
            pltpu.VMEM((length, columns), F32),
            pltpu.VMEM((length, columns), F32),
            pltpu.VMEM((length, columns), F32),
            pltpu.VMEM((2, length, columns), BF16),
            pltpu.VMEM((chips, rows, columns), BF16),
            pltpu.VMEM((chips, tall, wide, share, columns // 2), BF16),
            pltpu.VMEM((chips, tall, wide, share, columns // 2), BF16),
            pltpu.VMEM((chips, wide, share, columns // 2), BF16),
            pltpu.VMEM((chips, tall, share, columns // 2), BF16),
            pltpu.VMEM((wide, chips, share, columns), BF16),
            pltpu.VMEM((tall, chips, share, columns), BF16),
            pltpu.VMEM((chips, share, columns), BF16),
            pltpu.VMEM((chips, share, columns), BF16),
            pltpu.VMEM((rows, columns), BF16),
            pltpu.VMEM((2, 8, head_dim), F32),
            pltpu.VMEM((data, 8, head_dim), F32),
            pltpu.VMEM((chips, 8, head_dim), F32),
            dma((8,)),
            dma((3, chips)),
            dma((2, chips)),
            dma((2, chips, max(wide - 1, 1))),
            dma((2, chips, max(tall - 1, 1))),
            dma((2, chips, max(tall - 1, 1), max(wide - 1, 1))),
            dma((2, chips, max(tall - 1, 1), max(wide - 1, 1))),
            dma((6,)),
            dma((2, chips, max(tall - 1, 1), max(wide - 1, 1))),
            dma((2, chips, max(tall - 1, 1), max(wide - 1, 1))),
            dma((2, 2, chips, max(wide - 1, 1))),
            dma((2, 2, chips, max(tall - 1, 1))),
            dma((2, chips)),
            dma((2, data)),
            dma((2, data)),
            dma((2, chips)),
        ],
        compiler_params=pltpu.CompilerParams(
            collective_id=0, has_side_effects=True, vmem_limit_bytes=64 * 1024 * 1024
        ),
        cost_estimate=pl.CostEstimate(flops=2_000_000_000, bytes_accessed=6_000_000, transcendentals=300_000),
        name="kv_backward",
    )(
        hidden_row,
        queries[0],
        upstream[0],
        advantage,
        selected,
        segment,
        w_kv,
        k_gain.reshape(1, head_dim),
        q_gain.reshape(1, head_dim),
    )
    return (d_weight[:rows_dev].astype(F32), d_gain[0])


def solution(mesh):
    in_specs = (
        P(("dp", "fsdp"), None, None),
        P(("dp", "fsdp"), None, None),
        P(("dp", "fsdp"), None, None),
        P(("dp", "fsdp"), None),
        P(("dp", "fsdp"), None),
        P(("dp", "fsdp"), None),
        P("fsdp", None),
        P(),
        P(),
    )
    out_specs = (P("fsdp", None), P())
    data = mesh.shape["dp"]
    tall = max(n for n in range(1, math.isqrt(data) + 1) if data % n == 0)
    return jax.shard_map(
        functools.partial(shards, (tall, data // tall), mesh.shape["fsdp"]),
        mesh=mesh,
        in_specs=in_specs,
        out_specs=out_specs,
        check_vma=False,
    )
```

```python
import functools
import math

import jax
import jax.numpy as jnp
from jax import lax
from jax.experimental import pallas as pl
from jax.experimental.pallas import tpu as pltpu
from jax.sharding import PartitionSpec as P

CAP = 128
epsilon = 1e-06
MESH = pl.DeviceIdType.MESH
F32 = jnp.float32
BF16 = jnp.bfloat16


def dot_last(a, b):
    return lax.dot_general(a, b, (((1,), (1,)), ((), ())), preferred_element_type=F32)


def dot(a, b):
    return jnp.dot(a, b, preferred_element_type=F32)


def body(
    grid,
    owners,
    hidden,
    queries,
    upstream,
    advantage,
    selected,
    segment,
    w_own,
    k_gain,
    q_gain,
    d_weight,
    d_gain,
    adv_in,
    sel_in,
    seg_in,
    kg_in,
    qg_in,
    hid,
    hid_t,
    w_half,
    q_raw,
    u_raw,
    q_sel,
    c_sel,
    q_sel_t,
    c_sel_t,
    probs_all,
    probs_b,
    dscore_all,
    allowed,
    kv_out,
    kv_own,
    kv_in,
    d_kv,
    part,
    mid_row,
    mid_col,
    relay_row,
    relay_col,
    from_row,
    from_col,
    z_out,
    from_z,
    kept,
    final,
    gain_core,
    gain_data,
    gain_z,
    local_sem,
    hid_sem,
    swap_sem,
    w_z_sem,
    w_row_sem,
    w_col_sem,
    w_diag_row_sem,
    w_diag_col_sem,
    kv_sem,
    d_kv_sem,
    mid_row_sem,
    mid_col_sem,
    row_sem,
    col_sem,
    z_sem,
    final_sem,
    gain_core_sem,
    gain_data_sem,
    gain_z_sem,
):
    tall, wide = grid
    data = tall * wide
    chips = owners // 2
    rows = w_own.shape[0]
    share = rows // data
    length = hidden.shape[0]
    head_dim = k_gain.shape[1]
    heads = queries.shape[1] // head_dim
    cap = allowed.shape[1] // 2
    scale = head_dim ** (-0.5)
    key, value = 0, 1
    dp = lax.axis_index("dp")
    me = lax.axis_index("fsdp")
    chip = me // 2
    core = me % 2
    sibling = {"dp": dp, "fsdp": chip * 2 + 1 - core}
    row, col = dp // wide, dp % wide

    def chip_at(k):
        return lax.rem(chip + k, chips)

    def data_at(k):
        return lax.rem(dp + k, data)

    def place(s, t):
        return lax.rem(row + s, tall) * wide + lax.rem(col + t, wide)

    def to_chip(other):
        return {"dp": dp, "fsdp": other * 2 + core}

    def to_data(other):
        return {"dp": other, "fsdp": me}

    def rows_of(p):
        return pl.ds(pl.multiple_of(p * share, 16), share)

    def half_of(p, piece):
        return pl.ds(pl.multiple_of(p * share + piece * (share // 2), 16), share // 2)

    def lanes_of(c):
        return pl.ds(c * head_dim, head_dim)

    started = []

    def begin(src, dst, sems, at, device):
        copy = pltpu.make_async_remote_copy(
            src_ref=src,
            dst_ref=dst,
            send_sem=sems.at[(0, *at)],
            recv_sem=sems.at[(1, *at)],
            device_id=device,
            device_id_type=MESH,
        )
        copy.start()
        started.append(copy)
        return copy

    own_w = []
    for c in (key, value):
        load = pltpu.make_async_copy(w_own.at[:, lanes_of(c)], w_half.at[c, chip], local_sem.at[c])
        load.start()
        own_w.append(load)
    loads = []
    smalls = []
    for n, (src, dst) in enumerate(
        (
            (advantage, adv_in),
            (selected, sel_in),
            (segment, seg_in),
            (k_gain, kg_in),
            (q_gain, qg_in),
            (queries, q_raw),
            (upstream, u_raw),
        )
    ):
        load = pltpu.make_async_copy(src, dst, local_sem.at[2 + n])
        load.start()
        smalls.append(load)
    for j in range(chips):
        cols = pl.ds(pl.multiple_of((2 * j + core) * rows, 128), rows)
        load = pltpu.make_async_copy(hidden.at[:, cols], hid.at[0, :, pl.ds(j * rows, rows)], hid_sem.at[0, j])
        load.start()
        loads.append(load)

    barrier = pltpu.get_barrier_semaphore()
    pl.semaphore_signal(barrier, inc=1, device_id=sibling, device_id_type=MESH)
    for k in range(1, chips):
        pl.semaphore_signal(barrier, inc=1, device_id=to_chip(chip_at(k)), device_id_type=MESH)
    for k in range(1, data):
        pl.semaphore_signal(barrier, inc=1, device_id=to_data(data_at(k)), device_id_type=MESH)
    pl.semaphore_wait(barrier, chips + data - 1)

    mine = rows_of(dp)
    sends = {}

    def send_share(c):
        for k in range(1, chips):
            sends[c, k] = begin(
                w_own.at[mine, lanes_of(c)], w_half.at[c, chip, mine], w_z_sem, (c, k), to_chip(chip_at(k))
            )

    send_share(key)
    swaps = []
    for j in range(chips):
        cols = pl.ds(pl.multiple_of((2 * j + 1 - core) * rows, 128), rows)
        swaps.append(begin(hidden.at[:, cols], hid.at[1, :, pl.ds(j * rows, rows)], swap_sem, (j,), sibling))
    send_share(value)

    for load in smalls:
        load.wait()
    chosen = sel_in[...].astype(F32)
    places = lax.broadcasted_iota(jnp.int32, (length, length), 0)
    others = lax.broadcasted_iota(jnp.int32, (length, length), 1)
    upto = places <= others
    rank = dot(jnp.broadcast_to(chosen, (16, length)).astype(BF16), upto.astype(F32).astype(BF16))[:1]
    slots = lax.broadcasted_iota(jnp.int32, (cap, length), 0).astype(F32) + 1.0
    pick = jnp.where(rank == slots, chosen, 0.0)
    pick_b = pick.astype(BF16)
    token_weight = jnp.sum(pick * (adv_in[...] * chosen), axis=1, keepdims=True)
    groups = jnp.broadcast_to(seg_in[...].astype(F32), (length, length))
    allowed_full = jnp.where((groups == groups.T) & upto, 1.0, 0.0).astype(BF16)
    allowed_sel = dot_last(allowed_full, pick_b)
    allowed[:, :cap] = allowed_sel
    allowed[:, cap:] = allowed_sel

    near = {}
    diag = {}

    def forward(c, k):
        sends[c, k].wait_recv()
        block = w_half.at[c, chip_at(chips - k), mine]
        for t in range(1, wide):
            near[c, k, 0, t] = begin(block, block, w_row_sem, (c, k, t - 1), to_data(place(0, t)))
        for s in range(1, tall):
            near[c, k, s, 0] = begin(block, block, w_col_sem, (c, k, s - 1), to_data(place(s, 0)))

    def forward_diag(c, k):
        source = chip_at(chips - k)
        for t in range(1, wide):
            near[c, k, 0, t].wait_recv()
            for s in range(1, tall):
                block = w_half.at[c, source, half_of(place(0, wide - t), 0)]
                diag[c, k, 0, s, t] = begin(
                    block, block, w_diag_row_sem, (c, k, s - 1, t - 1), to_data(place(s, 0))
                )
        for s in range(1, tall):
            near[c, k, s, 0].wait_recv()
            for t in range(1, wide):
                block = w_half.at[c, source, half_of(place(tall - s, 0), 1)]
                diag[c, k, 1, s, t] = begin(
                    block, block, w_diag_col_sem, (c, k, s - 1, t - 1), to_data(place(0, t))
                )

    def prepare_head(h):
        lanes = pl.ds(h * head_dim, head_dim)
        rows_h = pl.ds(h * cap, cap)
        query = dot(pick_b, q_raw[:, lanes])
        query_scale = lax.rsqrt(jnp.mean(query * query, axis=-1, keepdims=True) + epsilon)
        query = query * query_scale * qg_in[...]
        q_sel[rows_h] = query.astype(BF16)
        q_sel_t[:, rows_h] = query.T.astype(BF16)
        grad = token_weight * dot(pick_b, u_raw[:, lanes])
        c_sel[rows_h] = grad.astype(BF16)
        c_sel_t[:, rows_h] = grad.T.astype(BF16)

    def turn_own(j):
        loads[j].wait()
        hid_t[pl.ds(j * rows, rows), :length] = hid[0, :, pl.ds(j * rows, rows)].T

    def turn_swapped(j):
        swaps[j].wait_recv()
        hid_t[pl.ds(j * rows, rows), length:] = hid[1, :, pl.ds(j * rows, rows)].T

    tasks = [functools.partial(prepare_head, h) for h in range(heads)]
    tasks += [functools.partial(turn_own, j) for j in range(chips)]
    tasks += [functools.partial(turn_swapped, j) for j in range(chips)]
    events = []
    for k in range(1, chips):
        events.append(functools.partial(forward, key, k))
        if k > 1:
            events.append(functools.partial(forward_diag, key, k - 1))
    if chips > 1:
        events.append(functools.partial(forward_diag, key, chips - 1))
        events.append(functools.partial(forward, value, 1))
    done = 0
    for n, event in enumerate(events):
        until = len(tasks) * (n + 1) // (len(events) + 1)
        for task in tasks[done:until]:
            task()
        done = until
        event()
    for task in tasks[done:]:
        task()

    def project(c):
        own_w[c].wait()
        for k in range(chips):
            source = chip_at(chips - k)
            for at in diag:
                if at[:2] == (c, k):
                    diag[at].wait_recv()
            cols = pl.ds(pl.multiple_of(source * rows, 128), rows)
            weight = w_half[c, source]
            if k == 0:
                kv_out[c] = dot(hid[1, :, cols], weight)
            else:
                kv_out[c] += dot(hid[1, :, cols], weight)
            if k == chips - 1:
                swap = begin(kv_out.at[c], kv_in.at[c], kv_sem, (c,), sibling)
            if k == 0:
                kv_own[c] = dot(hid[0, :, cols], weight)
            else:
                kv_own[c] += dot(hid[0, :, cols], weight)
        return swap

    swap_key = project(key)
    for k in range(2, chips):
        forward(value, k)
    for k in range(1, chips - 1):
        forward_diag(value, k)
    swap_key.wait_recv()
    k_raw = kv_own[key] + kv_in[key]
    k_scale = lax.rsqrt(jnp.mean(k_raw * k_raw, axis=-1, keepdims=True) + epsilon)
    k_hat = k_raw * k_scale
    k_norm = (k_hat * kg_in[...]).astype(BF16)

    for h in range(heads // 2):
        pair = pl.ds(h * 2 * cap, 2 * cap)
        expo = jnp.exp(dot(k_norm, q_sel_t[:, pair]) * scale) * allowed[...]
        total = jnp.sum(expo, axis=0, keepdims=True)
        probs = expo * (1.0 / jnp.where(total > 0.0, total, 1.0))
        probs_all[:, pair] = probs
        probs_b[:, pair] = probs.astype(BF16)
    d_kv[value, 0] = dot(probs_b[...], c_sel[...]).astype(BF16)
    swap_d = {value: begin(d_kv.at[value, 0], d_kv.at[value, 1], d_kv_sem, (value,), sibling)}
    if chips > 1:
        forward_diag(value, chips - 1)

    mids = {}
    nears = {}
    along = {}

    def make(c, k):
        target = chip_at(k)
        block = pl.ds(pl.multiple_of(target * rows, 128), rows)
        if k == 1:
            mixed = dot(hid_t[block, :length], d_kv[c, 0])
            swap_d[c].wait_recv()
            part[c, target] = (mixed + dot(hid_t[block, length:], d_kv[c, 1])).astype(BF16)
        else:
            part[c, target] = dot(hid_t[block, :], d_kv[c].reshape(2 * length, head_dim)).astype(BF16)
        at = (c, k - 1)
        for s in range(1, tall):
            for t in range(1, wide):
                far = place(s, t)
                mids[c, k, 0, s, t] = begin(
                    part.at[c, target, half_of(far, 0)],
                    mid_row.at[c, k - 1, s - 1, t - 1],
                    mid_row_sem,
                    (*at, s - 1, t - 1),
                    to_data(place(0, t)),
                )
                mids[c, k, 1, s, t] = begin(
                    part.at[c, target, half_of(far, 1)],
                    mid_col.at[c, k - 1, s - 1, t - 1],
                    mid_col_sem,
                    (*at, s - 1, t - 1),
                    to_data(place(s, 0)),
                )
        for t in range(1, wide):
            other = place(0, t)
            if tall == 1:
                source, into = part.at[c, target, rows_of(other)], from_row.at[c, t, k - 1]
            else:
                source = part.at[c, target, half_of(other, 0)]
                into = from_row.at[c, t, k - 1, pl.ds(0, share // 2)]
            nears[c, k, 0, t, 0] = begin(source, into, row_sem, (*at, 0, t - 1), to_data(other))
        for s in range(1, tall):
            other = place(s, 0)
            nears[c, k, s, 0, 1] = begin(
                part.at[c, target, half_of(other, 1)],
                from_col.at[c, s, k - 1, pl.ds(share // 2, share // 2)],
                col_sem,
                (*at, 0, s - 1),
                to_data(other),
            )

    def relay(c, k):
        target = chip_at(k)
        at = (c, k - 1)
        for s in range(1, tall):
            other = place(s, 0)
            sent = part[c, target, half_of(other, 0)].astype(F32)
            for t in range(1, wide):
                mids[c, k, 0, s, t].wait_recv()
                sent += mid_row[c, k - 1, s - 1, t - 1].astype(F32)
            relay_col[c, k - 1, s] = sent.astype(BF16)
            nears[c, k, s, 0, 0] = begin(
                relay_col.at[c, k - 1, s],
                from_col.at[c, s, k - 1, pl.ds(0, share // 2)],
                col_sem,
                (*at, 1, s - 1),
                to_data(other),
            )
        if tall == 1:
            return
        for t in range(1, wide):
            other = place(0, t)
            sent = part[c, target, half_of(other, 1)].astype(F32)
            for s in range(1, tall):
                mids[c, k, 1, s, t].wait_recv()
                sent += mid_col[c, k - 1, s - 1, t - 1].astype(F32)
            relay_row[c, k - 1, t] = sent.astype(BF16)
            nears[c, k, 0, t, 1] = begin(
                relay_row.at[c, k - 1, t],
                from_row.at[c, t, k - 1, pl.ds(share // 2, share // 2)],
                row_sem,
                (*at, 1, t - 1),
                to_data(other),
            )

    def collect(c, k):
        target = chip_at(k)
        for at in nears:
            if at[:2] == (c, k):
                nears[at].wait_recv()
        total = part[c, target, mine].astype(F32)
        for s in range(1, tall):
            total += from_col[c, s, k - 1].astype(F32)
        for t in range(1, wide):
            total += from_row[c, t, k - 1].astype(F32)
        if k < chips:
            z_out[c, k] = total.astype(BF16)
            along[c, k] = begin(z_out.at[c, k], from_z.at[c, k], z_sem, (c, k), to_chip(target))
        else:
            kept[c] = total

    finals = []

    def finish(c):
        total = kept[c]
        for k in range(1, chips):
            along[c, k].wait_recv()
            total += from_z[c, k].astype(F32)
        final[c, mine] = total.astype(BF16)
        for d in range(1, data):
            finals.append(begin(final.at[c, mine], final.at[c, mine], final_sem, (c, d), to_data(data_at(d))))

    swap_value = project(value)
    for k in range(1, chips + 1):
        make(value, k)
    swap_value.wait_recv()
    values = (kv_own[value] + kv_in[value]).astype(BF16)
    waiting = [functools.partial(relay, value, 1)]
    for k in range(2, chips + 1):
        waiting.append(functools.partial(relay, value, k))
        waiting.append(functools.partial(collect, value, k - 1))
    waiting.append(functools.partial(collect, value, chips))
    done = 0
    for h in range(heads // 2):
        pair = pl.ds(h * 2 * cap, 2 * cap)
        dprob = dot(values, c_sel_t[:, pair])
        delta = jnp.sum(probs_b[:, pair].astype(F32) * dprob, axis=0, keepdims=True)
        dscore_all[:, pair] = (probs_all[:, pair] * (dprob - delta) * scale).astype(BF16)
        until = (len(waiting) - 3) * (h + 1) // (heads // 2)
        for step in waiting[done:until]:
            step()
        done = max(done, until)
    d_key = dot(dscore_all[...], q_sel[...])
    d_khat = d_key * kg_in[...]
    d_kraw = k_scale * (d_khat - k_hat * jnp.mean(d_khat * k_hat, axis=-1, keepdims=True))
    d_kv[key, 0] = d_kraw.astype(BF16)
    swap_d[key] = begin(d_kv.at[key, 0], d_kv.at[key, 1], d_kv_sem, (key,), sibling)
    gain = jnp.sum(d_key * k_hat, axis=0, keepdims=True)
    gain_core[0] = jnp.broadcast_to(gain, (8, head_dim))
    swap_g = begin(gain_core.at[0], gain_core.at[1], gain_core_sem, (0,), sibling)
    for step in waiting[done:]:
        step()

    gains = []
    for k in range(1, chips + 3):
        if k <= chips:
            make(key, k)
        if k == 1:
            swap_g.wait_recv()
            gain_data[dp] = gain_core[0] + gain_core[1]
            for d in range(1, data):
                gains.append(begin(gain_data.at[dp], gain_data.at[dp], gain_data_sem, (d,), to_data(data_at(d))))
        if k == 2:
            finish(value)
        if 1 <= k - 1 <= chips:
            relay(key, k - 1)
        if 1 <= k - 2 <= chips:
            collect(key, k - 2)

    for copy in gains:
        copy.wait_recv()
    gain_sum = gain_data[0]
    for d in range(1, data):
        gain_sum += gain_data[d]
    gain_z[chip] = gain_sum
    z_gains = []
    for k in range(1, chips):
        z_gains.append(begin(gain_z.at[chip], gain_z.at[chip], gain_z_sem, (k,), to_chip(chip_at(k))))

    finish(key)
    for copy in z_gains:
        copy.wait_recv()
    gain_sum = gain_z[0]
    for k in range(1, chips):
        gain_sum += gain_z[k]
    d_gain[...] = gain_sum

    for copy in started:
        copy.wait_send()
    for copy in finals:
        copy.wait_recv()
    for c in (key, value):
        d_weight[:, lanes_of(c)] = final[c]


def shards(grid, owners, hidden, queries, upstream, advantage, selected, segment, w_kv, k_gain, q_gain):
    hidden_row = hidden[0]
    length, width = hidden_row.shape
    rows_dev, columns = w_kv.shape
    head_dim = k_gain.shape[0]
    heads = queries.shape[2] // head_dim
    tall, wide = grid
    data = tall * wide
    chips = owners // 2
    far_chips = chips if tall > 1 else 1
    far_rows = max(tall - 1, 1)
    far_cols = wide - 1 if tall > 1 else 1
    unit = math.lcm(128, 16 * data * min(tall, 2))
    rows = -(-rows_dev // unit) * unit
    share = rows // data
    if rows_dev * owners != width:
        hidden_row = jnp.pad(hidden_row, ((0, 0), (0, rows_dev * owners - width)))
    if rows != rows_dev:
        blocks = hidden_row.reshape(length, owners, rows_dev)
        hidden_row = jnp.pad(blocks, ((0, 0), (0, 0), (0, rows - rows_dev))).reshape(length, owners * rows)
        w_kv = jnp.pad(w_kv, ((0, rows - rows_dev), (0, 0)))
    vmem = pl.BlockSpec(memory_space=pltpu.VMEM)
    hbm = pl.BlockSpec(memory_space=pltpu.HBM)
    dma = pltpu.SemaphoreType.DMA
    d_weight, d_gain = pl.pallas_call(
        functools.partial(body, grid, owners),
        out_shape=(
            jax.ShapeDtypeStruct((rows, columns), BF16),
            jax.ShapeDtypeStruct((8, head_dim), F32),
        ),
        in_specs=[hbm] * 9,
        out_specs=(vmem, vmem),
        scratch_shapes=[
            pltpu.VMEM((1, length), F32),
            pltpu.VMEM((1, length), jnp.int32),
            pltpu.VMEM((1, length), jnp.int32),
            pltpu.VMEM((1, head_dim), F32),
            pltpu.VMEM((1, head_dim), F32),
            pltpu.VMEM((2, length, chips * rows), BF16),
            pltpu.VMEM((chips * rows, 2 * length), BF16),
            pltpu.VMEM((2, chips, rows, head_dim), BF16),
            pltpu.VMEM((length, heads * head_dim), BF16),
            pltpu.VMEM((length, heads * head_dim), BF16),
            pltpu.VMEM((heads * CAP, head_dim), BF16),
            pltpu.VMEM((heads * CAP, head_dim), BF16),
            pltpu.VMEM((head_dim, heads * CAP), BF16),
            pltpu.VMEM((head_dim, heads * CAP), BF16),
            pltpu.VMEM((length, heads * CAP), F32),
            pltpu.VMEM((length, heads * CAP), BF16),
            pltpu.VMEM((length, heads * CAP), BF16),
            pltpu.VMEM((length, 2 * CAP), F32),
            pltpu.VMEM((2, length, head_dim), F32),
            pltpu.VMEM((2, length, head_dim), F32),
            pltpu.VMEM((2, length, head_dim), F32),
            pltpu.VMEM((2, 2, length, head_dim), BF16),
            pltpu.VMEM((2, chips, rows, head_dim), BF16),
            pltpu.VMEM((2, far_chips, far_rows, far_cols, share // 2, head_dim), BF16),
            pltpu.VMEM((2, far_chips, far_rows, far_cols, share // 2, head_dim), BF16),
            pltpu.VMEM((2, chips, wide, share // 2, head_dim), BF16),
            pltpu.VMEM((2, chips, tall, share // 2, head_dim), BF16),
            pltpu.VMEM((2, wide, chips, share, head_dim), BF16),
            pltpu.VMEM((2, tall, chips, share, head_dim), BF16),
            pltpu.VMEM((2, chips, share, head_dim), BF16),
            pltpu.VMEM((2, chips, share, head_dim), BF16),
            pltpu.VMEM((2, share, head_dim), F32),
            pltpu.VMEM((2, rows, head_dim), BF16),
            pltpu.VMEM((2, 8, head_dim), F32),
            pltpu.VMEM((data, 8, head_dim), F32),
            pltpu.VMEM((chips, 8, head_dim), F32),
            dma((9,)),
            dma((1, chips)),
            dma((2, chips)),
            dma((2, 2, chips)),
            dma((2, 2, chips, max(wide - 1, 1))),
            dma((2, 2, far_chips, far_rows)),
            dma((2, 2, far_chips, far_rows, far_cols)),
            dma((2, 2, far_chips, far_rows, far_cols)),
            dma((2, 2)),
            dma((2, 2)),
            dma((2, 2, far_chips, far_rows, far_cols)),
            dma((2, 2, far_chips, far_rows, far_cols)),
            dma((2, 2, chips, min(tall, 2), max(wide - 1, 1))),
            dma((2, 2, far_chips, 2, far_rows)),
            dma((2, 2, chips)),
            dma((2, 2, data)),
            dma((2, 1)),
            dma((2, data)),
            dma((2, chips)),
        ],
        compiler_params=pltpu.CompilerParams(
            collective_id=0, has_side_effects=True, vmem_limit_bytes=64 * 1024 * 1024
        ),
        cost_estimate=pl.CostEstimate(flops=2_000_000_000, bytes_accessed=6_000_000, transcendentals=300_000),
        name="kv_backward",
    )(
        hidden_row,
        queries[0],
        upstream[0],
        advantage,
        selected,
        segment,
        w_kv,
        k_gain.reshape(1, head_dim),
        q_gain.reshape(1, head_dim),
    )
    return (d_weight[:rows_dev].astype(F32), d_gain[0])


def solution(mesh):
    in_specs = (
        P(("dp", "fsdp"), None, None),
        P(("dp", "fsdp"), None, None),
        P(("dp", "fsdp"), None, None),
        P(("dp", "fsdp"), None),
        P(("dp", "fsdp"), None),
        P(("dp", "fsdp"), None),
        P("fsdp", None),
        P(),
        P(),
    )
    out_specs = (P("fsdp", None), P())
    data = mesh.shape["dp"]
    tall = 2 if data == 4 else 1
    return jax.shard_map(
        functools.partial(shards, (tall, data // tall), mesh.shape["fsdp"]),
        mesh=mesh,
        in_specs=in_specs,
        out_specs=out_specs,
        check_vma=False,
    )
```

```python
import functools
import math

import jax
import jax.numpy as jnp
from jax import lax
from jax.experimental import pallas as pl
from jax.experimental.pallas import tpu as pltpu
from jax.sharding import PartitionSpec as P

CAP = 128
epsilon = 1e-06
MESH = pl.DeviceIdType.MESH
F32 = jnp.float32
BF16 = jnp.bfloat16


def dot_last(a, b):
    return lax.dot_general(a, b, (((1,), (1,)), ((), ())), preferred_element_type=F32)


def dot(a, b):
    return jnp.dot(a, b, preferred_element_type=F32)


def body(
    grid,
    owners,
    hidden,
    queries,
    upstream,
    advantage,
    selected,
    segment,
    w_own,
    k_gain,
    q_gain,
    d_weight,
    d_gain,
    adv_in,
    sel_in,
    seg_in,
    kg_in,
    qg_in,
    hid,
    hid_t,
    w_half,
    q_raw,
    u_raw,
    q_sel,
    c_sel,
    q_sel_t,
    c_sel_t,
    k_norm,
    values,
    probs_b,
    dscore_all,
    allowed,
    kv_out,
    kv_own,
    kv_in,
    d_kv,
    part,
    mid_row,
    mid_col,
    relay_row,
    relay_col,
    from_row,
    from_col,
    z_out,
    from_z,
    kept,
    final,
    gain_core,
    gain_data,
    gain_z,
    local_sem,
    hid_sem,
    swap_sem,
    w_z_sem,
    w_row_sem,
    w_col_sem,
    w_diag_row_sem,
    w_diag_col_sem,
    kv_sem,
    d_kv_sem,
    mid_row_sem,
    mid_col_sem,
    row_sem,
    col_sem,
    z_sem,
    final_sem,
    gain_core_sem,
    gain_data_sem,
    gain_z_sem,
):
    tall, wide = grid
    data = tall * wide
    chips = owners // 2
    rows = w_own.shape[0]
    share = rows // data
    length = hidden.shape[0]
    head_dim = k_gain.shape[1]
    heads = queries.shape[1] // head_dim
    cap = allowed.shape[1] // 2
    scale = head_dim ** (-0.5)
    dp = lax.axis_index("dp")
    me = lax.axis_index("fsdp")
    chip = me // 2
    core = me % 2
    sibling = {"dp": dp, "fsdp": chip * 2 + 1 - core}
    row, col = dp // wide, dp % wide

    def chip_at(k):
        return lax.rem(chip + k, chips)

    def data_at(k):
        return lax.rem(dp + k, data)

    def place(s, t):
        return lax.rem(row + s, tall) * wide + lax.rem(col + t, wide)

    def to_chip(other):
        return {"dp": dp, "fsdp": other * 2 + core}

    def to_data(other):
        return {"dp": other, "fsdp": me}

    def rows_of(p):
        return pl.ds(pl.multiple_of(p * share, 16), share)

    def half_of(p, piece):
        return pl.ds(pl.multiple_of(p * share + piece * (share // 2), 16), share // 2)

    def remote(src, dst, sems, at, device):
        return pltpu.make_async_remote_copy(
            src_ref=src,
            dst_ref=dst,
            send_sem=sems.at[(0, *at)],
            recv_sem=sems.at[(1, *at)],
            device_id=device,
            device_id_type=MESH,
        )

    started = []

    def begin(*args):
        copy = remote(*args)
        copy.start()
        started.append(copy)
        return copy

    def loop(low, high, step):
        def run(i, carry):
            step(i)
            return carry

        lax.fori_loop(low, high, run, 0)

    own_w = pltpu.make_async_copy(w_own, w_half.at[chip], local_sem.at[0])
    own_w.start()
    smalls = []
    for n, (src, dst) in enumerate(
        (
            (advantage, adv_in),
            (selected, sel_in),
            (segment, seg_in),
            (k_gain, kg_in),
            (q_gain, qg_in),
            (queries, q_raw),
            (upstream, u_raw),
        )
    ):
        load = pltpu.make_async_copy(src, dst, local_sem.at[2 + n])
        load.start()
        smalls.append(load)

    def block_of(j):
        return pl.ds(pl.multiple_of(j * rows, 128), rows)

    def load_hidden(j):
        return pltpu.make_async_copy(
            hidden.at[:, block_of(2 * j + core)], hid.at[0, :, block_of(j)], hid_sem.at[0, j]
        )

    def swap_hidden(j):
        return remote(
            hidden.at[:, block_of(2 * j + 1 - core)], hid.at[1, :, block_of(j)], swap_sem, (j,), sibling
        )

    loop(0, chips, lambda j: load_hidden(j).start())

    barrier = pltpu.get_barrier_semaphore()
    pl.semaphore_signal(barrier, inc=1, device_id=sibling, device_id_type=MESH)
    for k in range(1, chips):
        pl.semaphore_signal(barrier, inc=1, device_id=to_chip(chip_at(k)), device_id_type=MESH)
    for k in range(1, data):
        pl.semaphore_signal(barrier, inc=1, device_id=to_data(data_at(k)), device_id_type=MESH)
    pl.semaphore_wait(barrier, chips + data - 1)

    mine = rows_of(dp)
    sends = {}
    for k in range(1, chips):
        sends[k] = begin(w_own.at[mine], w_half.at[chip, mine], w_z_sem, (k,), to_chip(chip_at(k)))
    loop(0, chips, lambda j: swap_hidden(j).start())

    for load in smalls:
        load.wait()
    chosen = sel_in[...].astype(F32)
    places = lax.broadcasted_iota(jnp.int32, (length, length), 0)
    others = lax.broadcasted_iota(jnp.int32, (length, length), 1)
    upto = places <= others
    rank = dot(jnp.broadcast_to(chosen, (16, length)).astype(BF16), upto.astype(F32).astype(BF16))[:1]
    slots = lax.broadcasted_iota(jnp.int32, (cap, length), 0).astype(F32) + 1.0
    pick = jnp.where(rank == slots, chosen, 0.0)
    pick_b = pick.astype(BF16)
    token_weight = jnp.sum(pick * (adv_in[...] * chosen), axis=1, keepdims=True)
    groups = jnp.broadcast_to(seg_in[...].astype(F32), (length, length))
    allowed_full = jnp.where((groups == groups.T) & upto, 1.0, 0.0).astype(BF16)
    allowed_sel = dot_last(allowed_full, pick_b)
    allowed[:, :cap] = allowed_sel
    allowed[:, cap:] = allowed_sel

    near = {}
    diag = {}

    def forward(k):
        sends[k].wait_recv()
        block = w_half.at[chip_at(chips - k), mine]
        for t in range(1, wide):
            near[k, 0, t] = begin(block, block, w_row_sem, (k, t - 1), to_data(place(0, t)))
        for s in range(1, tall):
            near[k, s, 0] = begin(block, block, w_col_sem, (k, s - 1), to_data(place(s, 0)))

    def forward_diag(k):
        source = chip_at(chips - k)
        for t in range(1, wide):
            near[k, 0, t].wait_recv()
            for s in range(1, tall):
                block = w_half.at[source, half_of(place(0, wide - t), 0)]
                diag[k, 0, s, t] = begin(
                    block, block, w_diag_row_sem, (k, s - 1, t - 1), to_data(place(s, 0))
                )
        for s in range(1, tall):
            near[k, s, 0].wait_recv()
            for t in range(1, wide):
                block = w_half.at[source, half_of(place(tall - s, 0), 1)]
                diag[k, 1, s, t] = begin(
                    block, block, w_diag_col_sem, (k, s - 1, t - 1), to_data(place(0, t))
                )

    def prepare_head(h):
        lanes = pl.ds(pl.multiple_of(h * head_dim, 128), head_dim)
        rows_h = pl.ds(pl.multiple_of(h * cap, 128), cap)
        query = dot(pick_b, q_raw[:, lanes])
        query_scale = lax.rsqrt(jnp.mean(query * query, axis=-1, keepdims=True) + epsilon)
        query = query * query_scale * qg_in[...]
        q_sel[rows_h] = query.astype(BF16)
        q_sel_t[:, rows_h] = query.T.astype(BF16)
        grad = token_weight * dot(pick_b, u_raw[:, lanes])
        c_sel[rows_h] = grad.astype(BF16)
        c_sel_t[:, rows_h] = grad.T.astype(BF16)

    def turn_own(j):
        load_hidden(j).wait()
        hid_t[block_of(j), :length] = hid[0, :, block_of(j)].T

    def turn_swapped(j):
        swap_hidden(j).wait_recv()
        hid_t[block_of(j), length:] = hid[1, :, block_of(j)].T

    tasks = [
        functools.partial(loop, 0, heads // 2, prepare_head),
        functools.partial(loop, heads // 2, heads, prepare_head),
        functools.partial(loop, 0, chips, turn_own),
        functools.partial(loop, 0, chips, turn_swapped),
    ]
    events = []
    for k in range(1, chips):
        events.append(functools.partial(forward, k))
        if k > 1:
            events.append(functools.partial(forward_diag, k - 1))
    if chips > 1:
        events.append(functools.partial(forward_diag, chips - 1))
    done = 0
    for n, event in enumerate(events):
        until = len(tasks) * (n + 1) // (len(events) + 1)
        for task in tasks[done:until]:
            task()
        done = until
        event()
    for task in tasks[done:]:
        task()

    own_w.wait()
    for at in near:
        if tall == 1:
            near[at].wait_recv()
    for at in diag:
        diag[at].wait_recv()
    kv_out[...] = jnp.zeros_like(kv_out)
    kv_own[...] = jnp.zeros_like(kv_own)

    def project_swapped(j):
        kv_out[...] += dot(hid[1, :, block_of(j)], w_half[j])

    def project_own(j):
        kv_own[...] += dot(hid[0, :, block_of(j)], w_half[j])

    loop(0, chips, project_swapped)
    swap_kv = begin(kv_out, kv_in, kv_sem, (), sibling)
    loop(0, chips, project_own)
    swap_kv.wait_recv()
    key_value = kv_own[...] + kv_in[...]
    k_raw = key_value[:, :head_dim]
    k_scale = lax.rsqrt(jnp.mean(k_raw * k_raw, axis=-1, keepdims=True) + epsilon)
    k_hat = k_raw * k_scale
    k_norm[...] = (k_hat * kg_in[...]).astype(BF16)
    values[...] = key_value[:, head_dim:].astype(BF16)

    def attend(h):
        pair = pl.ds(pl.multiple_of(h * 2 * cap, 128), 2 * cap)
        expo = jnp.exp(dot(k_norm[...], q_sel_t[:, pair]) * scale) * allowed[...]
        total = jnp.sum(expo, axis=0, keepdims=True)
        probs = expo * (1.0 / jnp.where(total > 0.0, total, 1.0))
        rounded = probs.astype(BF16)
        probs_b[:, pair] = rounded
        dprob = dot(values[...], c_sel_t[:, pair])
        delta = jnp.sum(rounded.astype(F32) * dprob, axis=0, keepdims=True)
        dscore_all[:, pair] = (probs * (dprob - delta) * scale).astype(BF16)

    loop(0, heads // 2, attend)
    d_key = dot(dscore_all[...], q_sel[...])
    d_khat = d_key * kg_in[...]
    d_kraw = k_scale * (d_khat - k_hat * jnp.mean(d_khat * k_hat, axis=-1, keepdims=True))
    d_kv[0, :, :head_dim] = d_kraw.astype(BF16)
    d_kv[0, :, head_dim:] = dot(probs_b[...], c_sel[...]).astype(BF16)
    swap_d = begin(d_kv.at[0], d_kv.at[1], d_kv_sem, (), sibling)
    gain = jnp.sum(d_key * k_hat, axis=0, keepdims=True)
    gain_core[0] = jnp.broadcast_to(gain, (8, head_dim))
    swap_g = begin(gain_core.at[0], gain_core.at[1], gain_core_sem, (0,), sibling)

    def mids(k):
        target = chip_at(k)
        copies = []
        for s in range(1, tall):
            for t in range(1, wide):
                far = place(s, t)
                copies.append(
                    remote(
                        part.at[target, half_of(far, 0)],
                        mid_row.at[k - 1, s - 1, t - 1],
                        mid_row_sem,
                        (k - 1, s - 1, t - 1),
                        to_data(place(0, t)),
                    )
                )
                copies.append(
                    remote(
                        part.at[target, half_of(far, 1)],
                        mid_col.at[k - 1, s - 1, t - 1],
                        mid_col_sem,
                        (k - 1, s - 1, t - 1),
                        to_data(place(s, 0)),
                    )
                )
        return copies

    def nears(k):
        target = chip_at(k)
        copies = []
        for t in range(1, wide):
            other = place(0, t)
            if tall == 1:
                source, into = part.at[target, rows_of(other)], from_row.at[t, k - 1]
            else:
                source = part.at[target, half_of(other, 0)]
                into = from_row.at[t, k - 1, pl.ds(0, share // 2)]
            copies.append(remote(source, into, row_sem, (k - 1, 0, t - 1), to_data(other)))
        for s in range(1, tall):
            other = place(s, 0)
            into = from_col.at[s, k - 1, pl.ds(share // 2, share // 2)]
            copies.append(
                remote(part.at[target, half_of(other, 1)], into, col_sem, (k - 1, 0, s - 1), to_data(other))
            )
        return copies

    def relays(k):
        copies = []
        for s in range(1, tall):
            into = from_col.at[s, k - 1, pl.ds(0, share // 2)]
            copies.append(
                remote(relay_col.at[k - 1, s], into, col_sem, (k - 1, 1, s - 1), to_data(place(s, 0)))
            )
        for t in range(1, wide):
            if tall > 1:
                into = from_row.at[t, k - 1, pl.ds(share // 2, share // 2)]
                copies.append(
                    remote(relay_row.at[k - 1, t], into, row_sem, (k - 1, 1, t - 1), to_data(place(0, t)))
                )
        return copies

    def along(k):
        return remote(z_out.at[k], from_z.at[k], z_sem, (k,), to_chip(chip_at(k)))

    def make(k):
        target = chip_at(k)
        both = d_kv[...].reshape(2 * length, 2 * head_dim)
        part[target] = dot(hid_t[block_of(target), :], both).astype(BF16)
        for copy in mids(k) + nears(k):
            copy.start()

    def relay(k):
        target = chip_at(k)
        for copy in mids(k):
            copy.wait_recv()
        for s in range(1, tall):
            sent = part[target, half_of(place(s, 0), 0)].astype(F32)
            for t in range(1, wide):
                sent += mid_row[k - 1, s - 1, t - 1].astype(F32)
            relay_col[k - 1, s] = sent.astype(BF16)
        for t in range(1, wide):
            if tall > 1:
                sent = part[target, half_of(place(0, t), 1)].astype(F32)
                for s in range(1, tall):
                    sent += mid_col[k - 1, s - 1, t - 1].astype(F32)
                relay_row[k - 1, t] = sent.astype(BF16)
        for copy in relays(k):
            copy.start()

    def collect(k):
        target = chip_at(k)
        for copy in nears(k) + relays(k):
            copy.wait_recv()
        total = part[target, mine].astype(F32)
        for s in range(1, tall):
            total += from_col[s, k - 1].astype(F32)
        for t in range(1, wide):
            total += from_row[t, k - 1].astype(F32)
        kept[...] = total

        @pl.when(k < chips)
        def _():
            z_out[k] = total.astype(BF16)
            along(k).start()

    swap_d.wait_recv()
    swap_g.wait_recv()
    gain_data[dp] = gain_core[0] + gain_core[1]
    gains = []
    for d in range(1, data):
        gains.append(begin(gain_data.at[dp], gain_data.at[dp], gain_data_sem, (d,), to_data(data_at(d))))

    def reduce_step(k):
        pl.when(k <= chips)(lambda: make(k))
        pl.when((k >= 2) & (k <= chips + 1))(lambda: relay(k - 1))
        pl.when(k >= 3)(lambda: collect(k - 2))

    loop(1, chips + 3, reduce_step)

    for copy in gains:
        copy.wait_recv()
    gain_sum = gain_data[0]
    for d in range(1, data):
        gain_sum += gain_data[d]
    gain_z[chip] = gain_sum
    z_gains = []
    for k in range(1, chips):
        z_gains.append(begin(gain_z.at[chip], gain_z.at[chip], gain_z_sem, (k,), to_chip(chip_at(k))))

    summed = kept[...]
    for k in range(1, chips):
        along(k).wait_recv()
        summed += from_z[k].astype(F32)
    final[mine] = summed.astype(BF16)
    finals = []
    for d in range(1, data):
        finals.append(begin(final.at[mine], final.at[mine], final_sem, (d,), to_data(data_at(d))))

    for copy in z_gains:
        copy.wait_recv()
    gain_sum = gain_z[0]
    for k in range(1, chips):
        gain_sum += gain_z[k]
    d_gain[...] = gain_sum

    def drain(k):
        for copy in mids(k) + nears(k) + relays(k):
            copy.wait_send()

    loop(0, chips, lambda j: swap_hidden(j).wait_send())
    loop(1, chips + 1, drain)
    loop(1, chips, lambda k: along(k).wait_send())
    for copy in started:
        copy.wait_send()
    for copy in finals:
        copy.wait_recv()
    d_weight[...] = final[...]


def shards(grid, owners, hidden, queries, upstream, advantage, selected, segment, w_kv, k_gain, q_gain):
    hidden_row = hidden[0]
    length, width = hidden_row.shape
    rows_dev, columns = w_kv.shape
    head_dim = k_gain.shape[0]
    heads = queries.shape[2] // head_dim
    tall, wide = grid
    data = tall * wide
    chips = owners // 2
    far_chips = chips if tall > 1 else 1
    far_rows = max(tall - 1, 1)
    far_cols = wide - 1 if tall > 1 else 1
    unit = math.lcm(128, 16 * data * min(tall, 2))
    rows = -(-rows_dev // unit) * unit
    share = rows // data
    if rows_dev * owners != width:
        hidden_row = jnp.pad(hidden_row, ((0, 0), (0, rows_dev * owners - width)))
    if rows != rows_dev:
        blocks = hidden_row.reshape(length, owners, rows_dev)
        hidden_row = jnp.pad(blocks, ((0, 0), (0, 0), (0, rows - rows_dev))).reshape(length, owners * rows)
        w_kv = jnp.pad(w_kv, ((0, rows - rows_dev), (0, 0)))
    vmem = pl.BlockSpec(memory_space=pltpu.VMEM)
    hbm = pl.BlockSpec(memory_space=pltpu.HBM)
    dma = pltpu.SemaphoreType.DMA
    d_weight, d_gain = pl.pallas_call(
        functools.partial(body, grid, owners),
        out_shape=(
            jax.ShapeDtypeStruct((rows, columns), BF16),
            jax.ShapeDtypeStruct((8, head_dim), F32),
        ),
        in_specs=[hbm] * 9,
        out_specs=(vmem, vmem),
        scratch_shapes=[
            pltpu.VMEM((1, length), F32),
            pltpu.VMEM((1, length), jnp.int32),
            pltpu.VMEM((1, length), jnp.int32),
            pltpu.VMEM((1, head_dim), F32),
            pltpu.VMEM((1, head_dim), F32),
            pltpu.VMEM((2, length, chips * rows), BF16),
            pltpu.VMEM((chips * rows, 2 * length), BF16),
            pltpu.VMEM((chips, rows, columns), BF16),
            pltpu.VMEM((length, heads * head_dim), BF16),
            pltpu.VMEM((length, heads * head_dim), BF16),
            pltpu.VMEM((heads * CAP, head_dim), BF16),
            pltpu.VMEM((heads * CAP, head_dim), BF16),
            pltpu.VMEM((head_dim, heads * CAP), BF16),
            pltpu.VMEM((head_dim, heads * CAP), BF16),
            pltpu.VMEM((length, head_dim), BF16),
            pltpu.VMEM((length, head_dim), BF16),
            pltpu.VMEM((length, heads * CAP), BF16),
            pltpu.VMEM((length, heads * CAP), BF16),
            pltpu.VMEM((length, 2 * CAP), F32),
            pltpu.VMEM((length, columns), F32),
            pltpu.VMEM((length, columns), F32),
            pltpu.VMEM((length, columns), F32),
            pltpu.VMEM((2, length, columns), BF16),
            pltpu.VMEM((chips, rows, columns), BF16),
            pltpu.VMEM((far_chips, far_rows, far_cols, share // 2, columns), BF16),
            pltpu.VMEM((far_chips, far_rows, far_cols, share // 2, columns), BF16),
            pltpu.VMEM((chips, wide, share // 2, columns), BF16),
            pltpu.VMEM((chips, tall, share // 2, columns), BF16),
            pltpu.VMEM((wide, chips, share, columns), BF16),
            pltpu.VMEM((tall, chips, share, columns), BF16),
            pltpu.VMEM((chips, share, columns), BF16),
            pltpu.VMEM((chips, share, columns), BF16),
            pltpu.VMEM((share, columns), F32),
            pltpu.VMEM((rows, columns), BF16),
            pltpu.VMEM((2, 8, head_dim), F32),
            pltpu.VMEM((data, 8, head_dim), F32),
            pltpu.VMEM((chips, 8, head_dim), F32),
            dma((9,)),
            dma((1, chips)),
            dma((2, chips)),
            dma((2, chips)),
            dma((2, chips, max(wide - 1, 1))),
            dma((2, far_chips, far_rows)),
            dma((2, far_chips, far_rows, far_cols)),
            dma((2, far_chips, far_rows, far_cols)),
            dma((2,)),
            dma((2,)),
            dma((2, far_chips, far_rows, far_cols)),
            dma((2, far_chips, far_rows, far_cols)),
            dma((2, chips, min(tall, 2), max(wide - 1, 1))),
            dma((2, far_chips, 2, far_rows)),
            dma((2, chips)),
            dma((2, data)),
            dma((2, 1)),
            dma((2, data)),
            dma((2, chips)),
        ],
        compiler_params=pltpu.CompilerParams(
            collective_id=0, has_side_effects=True, vmem_limit_bytes=64 * 1024 * 1024
        ),
        cost_estimate=pl.CostEstimate(flops=2_000_000_000, bytes_accessed=6_000_000, transcendentals=300_000),
        name="kv_backward",
    )(
        hidden_row,
        queries[0],
        upstream[0],
        advantage,
        selected,
        segment,
        w_kv,
        k_gain.reshape(1, head_dim),
        q_gain.reshape(1, head_dim),
    )
    return (d_weight[:rows_dev].astype(F32), d_gain[0])


def solution(mesh):
    in_specs = (
        P(("dp", "fsdp"), None, None),
        P(("dp", "fsdp"), None, None),
        P(("dp", "fsdp"), None, None),
        P(("dp", "fsdp"), None),
        P(("dp", "fsdp"), None),
        P(("dp", "fsdp"), None),
        P("fsdp", None),
        P(),
        P(),
    )
    out_specs = (P("fsdp", None), P())
    data = mesh.shape["dp"]
    tall = 2 if data == 4 else 1
    return jax.shard_map(
        functools.partial(shards, (tall, data // tall), mesh.shape["fsdp"]),
        mesh=mesh,
        in_specs=in_specs,
        out_specs=out_specs,
        check_vma=False,
    )
```

```python
import functools
import math

import jax
import jax.numpy as jnp
from jax import lax
from jax.experimental import pallas as pl
from jax.experimental.pallas import tpu as pltpu
from jax.sharding import PartitionSpec as P

CAP = 128
epsilon = 1e-06
MESH = pl.DeviceIdType.MESH
F32 = jnp.float32
BF16 = jnp.bfloat16


def dot_last(a, b):
    return lax.dot_general(a, b, (((1,), (1,)), ((), ())), preferred_element_type=F32)


def dot(a, b):
    return jnp.dot(a, b, preferred_element_type=F32)


def body(
    grid,
    owners,
    hidden,
    queries,
    upstream,
    advantage,
    selected,
    segment,
    w_own,
    k_gain,
    q_gain,
    d_weight,
    d_gain,
    adv_in,
    sel_in,
    seg_in,
    kg_in,
    qg_in,
    hid,
    hid_t,
    w_half,
    q_raw,
    u_raw,
    q_sel,
    c_sel,
    q_sel_t,
    c_sel_t,
    probs_all,
    dscore_all,
    allowed,
    kv_out,
    kv_own,
    kv_in,
    d_kv,
    part,
    mid_row,
    mid_col,
    relay_row,
    relay_col,
    from_row,
    from_col,
    z_out,
    from_z,
    final,
    gain_core,
    gain_data,
    gain_z,
    local_sem,
    hid_sem,
    w_z_sem,
    w_row_sem,
    w_col_sem,
    w_diag_row_sem,
    w_diag_col_sem,
    core_sem,
    mid_row_sem,
    mid_col_sem,
    row_sem,
    col_sem,
    z_sem,
    final_sem,
    gain_data_sem,
    gain_z_sem,
):
    tall, wide = grid
    data = tall * wide
    chips = owners // 2
    rows = w_own.shape[0]
    share = rows // data
    length = hidden.shape[0]
    head_dim = k_gain.shape[1]
    half = w_own.shape[1] // 2
    low, high = pl.ds(0, half), pl.ds(half, half)
    heads = queries.shape[1] // head_dim
    cap = allowed.shape[1] // 2
    scale = head_dim ** (-0.5)
    dp = lax.axis_index("dp")
    me = lax.axis_index("fsdp")
    chip = me // 2
    core = me % 2
    sibling = {"dp": dp, "fsdp": chip * 2 + 1 - core}

    def chip_at(k):
        return lax.rem(chip + k, chips)

    def data_at(k):
        return lax.rem(dp + k, data)

    row, col = dp // wide, dp % wide

    def place(s, t):
        return lax.rem(row + s, tall) * wide + lax.rem(col + t, wide)

    def to_chip(other):
        return {"dp": dp, "fsdp": other * 2 + core}

    def to_data(other):
        return {"dp": other, "fsdp": me}

    def rows_of(p):
        return pl.ds(pl.multiple_of(p * share, 16), share)

    def remote(src, dst, send, recv, device):
        return pltpu.make_async_remote_copy(
            src_ref=src, dst_ref=dst, send_sem=send, recv_sem=recv, device_id=device, device_id_type=MESH
        )

    own_w = pltpu.make_async_copy(w_own, w_half.at[chip], local_sem.at[0])
    own_w.start()
    load_q = pltpu.make_async_copy(queries, q_raw, local_sem.at[1])
    load_q.start()
    load_u = pltpu.make_async_copy(upstream, u_raw, local_sem.at[2])
    load_u.start()
    smalls = []
    for n, (src, dst) in enumerate(
        ((advantage, adv_in), (selected, sel_in), (segment, seg_in), (k_gain, kg_in), (q_gain, qg_in))
    ):
        load = pltpu.make_async_copy(src, dst, local_sem.at[3 + n])
        load.start()
        smalls.append(load)
    loads = []
    for j in range(chips):
        cols = pl.ds(pl.multiple_of((2 * j + core) * rows, 128), rows)
        load = pltpu.make_async_copy(
            hidden.at[:, cols], hid.at[0, :, pl.ds(j * rows, rows)], hid_sem.at[0, j]
        )
        load.start()
        loads.append(load)

    barrier = pltpu.get_barrier_semaphore()
    pl.semaphore_signal(barrier, inc=1, device_id=sibling, device_id_type=MESH)
    for k in range(1, chips):
        pl.semaphore_signal(barrier, inc=1, device_id=to_chip(chip_at(k)), device_id_type=MESH)
    for k in range(1, data):
        pl.semaphore_signal(barrier, inc=1, device_id=to_data(data_at(k)), device_id_type=MESH)
    pl.semaphore_wait(barrier, chips + data - 1)

    mine = rows_of(dp)
    sends = []
    for k in range(1, chips):
        copy = remote(
            w_own.at[mine], w_half.at[chip, mine], w_z_sem.at[0, k], w_z_sem.at[1, k], to_chip(chip_at(k))
        )
        copy.start()
        sends.append(copy)
    swaps = []
    for j in range(chips):
        cols = pl.ds(pl.multiple_of((2 * j + 1 - core) * rows, 128), rows)
        copy = remote(
            hidden.at[:, cols],
            hid.at[1, :, pl.ds(j * rows, rows)],
            hid_sem.at[1, j],
            hid_sem.at[2, j],
            sibling,
        )
        copy.start()
        swaps.append(copy)

    for load in smalls:
        load.wait()
    chosen = sel_in[...].astype(F32)
    places = lax.broadcasted_iota(jnp.int32, (length, length), 0)
    others = lax.broadcasted_iota(jnp.int32, (length, length), 1)
    upto = places <= others
    rank = dot(jnp.broadcast_to(chosen, (16, length)).astype(BF16), upto.astype(F32).astype(BF16))[:1]
    slots = lax.broadcasted_iota(jnp.int32, (cap, length), 0).astype(F32) + 1.0
    pick = jnp.where(rank == slots, chosen, 0.0)
    pick_b = pick.astype(BF16)
    token_weight = jnp.sum(pick * (adv_in[...] * chosen), axis=1, keepdims=True)
    groups = jnp.broadcast_to(seg_in[...].astype(F32), (length, length))
    allowed_full = jnp.where((groups == groups.T) & upto, 1.0, 0.0).astype(BF16)
    allowed_sel = dot_last(allowed_full, pick_b)
    allowed[:, :cap] = allowed_sel
    allowed[:, cap:] = allowed_sel

    ahead = []
    near = {}
    diag = {}

    def forward(k):
        sends[k - 1].wait_recv()
        source = chip_at(chips - k)
        for t in range(1, wide):
            near[k, 0, t] = remote(
                w_half.at[source, mine],
                w_half.at[source, mine],
                w_row_sem.at[0, k, t - 1],
                w_row_sem.at[1, k, t - 1],
                to_data(place(0, t)),
            )
        for s in range(1, tall):
            near[k, s, 0] = remote(
                w_half.at[source, mine],
                w_half.at[source, mine],
                w_col_sem.at[0, k, s - 1],
                w_col_sem.at[1, k, s - 1],
                to_data(place(s, 0)),
            )
        for copy in [near[key] for key in near if key[0] == k]:
            copy.start()
            ahead.append(copy)

    def forward_diag(k):
        source = chip_at(chips - k)
        for t in range(1, wide):
            near[k, 0, t].wait_recv()
            block = w_half.at[source, rows_of(place(0, wide - t)), low]
            for s in range(1, tall):
                diag[k, 0, s, t] = remote(
                    block, block, w_diag_row_sem.at[0, k, s - 1, t - 1], w_diag_row_sem.at[1, k, s - 1, t - 1], to_data(place(s, 0))
                )
                diag[k, 0, s, t].start()
                ahead.append(diag[k, 0, s, t])
        for s in range(1, tall):
            near[k, s, 0].wait_recv()
            block = w_half.at[source, rows_of(place(tall - s, 0)), high]
            for t in range(1, wide):
                diag[k, 1, s, t] = remote(
                    block, block, w_diag_col_sem.at[0, k, s - 1, t - 1], w_diag_col_sem.at[1, k, s - 1, t - 1], to_data(place(0, t))
                )
                diag[k, 1, s, t].start()
                ahead.append(diag[k, 1, s, t])

    def prepare_head(h):
        lanes = pl.ds(h * head_dim, head_dim)
        rows_h = pl.ds(h * cap, cap)
        query = dot(pick_b, q_raw[:, lanes])
        query_scale = lax.rsqrt(jnp.mean(query * query, axis=-1, keepdims=True) + epsilon)
        query = query * query_scale * qg_in[...]
        q_sel[rows_h] = query.astype(BF16)
        q_sel_t[:, rows_h] = query.T.astype(BF16)
        grad = token_weight * dot(pick_b, u_raw[:, lanes])
        c_sel[rows_h] = grad.astype(BF16)
        c_sel_t[:, rows_h] = grad.T.astype(BF16)

    def turn_own(j):
        loads[j].wait()
        hid_t[pl.ds(j * rows, rows), :length] = hid[0, :, pl.ds(j * rows, rows)].T

    def turn_swapped(j):
        swaps[j].wait()
        hid_t[pl.ds(j * rows, rows), length:] = hid[1, :, pl.ds(j * rows, rows)].T

    tasks = [functools.partial(prepare_head, h) for h in range(heads)]
    tasks += [functools.partial(turn_own, j) for j in range(chips)]
    tasks += [functools.partial(turn_swapped, j) for j in range(chips)]
    events = []
    for k in range(1, chips):
        events.append(functools.partial(forward, k))
        if k > 1:
            events.append(functools.partial(forward_diag, k - 1))
    if chips > 1:
        events.append(functools.partial(forward_diag, chips - 1))
    load_q.wait()
    load_u.wait()
    done = 0
    for n, event in enumerate(events):
        until = len(tasks) * (n + 1) // (len(events) + 1)
        for task in tasks[done:until]:
            task()
        done = until
        event()
    for task in tasks[done:]:
        task()

    own_w.wait()
    for k in range(chips):
        source = chip_at(chips - k)
        for key in diag:
            if key[0] == k:
                diag[key].wait_recv()
        cols = pl.ds(pl.multiple_of(source * rows, 128), rows)
        weight = w_half[source]
        if k == 0:
            kv_out[...] = dot(hid[1, :, cols], weight)
            kv_own[...] = dot(hid[0, :, cols], weight)
        elif k < chips - 1:
            kv_out[...] += dot(hid[1, :, cols], weight)
            kv_own[...] += dot(hid[0, :, cols], weight)
        else:
            kv_out[...] += dot(hid[1, :, cols], weight)
    swap_kv = remote(kv_out, kv_in, core_sem.at[0], core_sem.at[1], sibling)
    swap_kv.start()
    key_value = kv_own[...]
    if chips > 1:
        key_value += dot(hid[0, :, cols], weight)
    swap_kv.wait()
    key_value = key_value + kv_in[...]

    k_raw = key_value[:, :head_dim]
    k_scale = lax.rsqrt(jnp.mean(k_raw * k_raw, axis=-1, keepdims=True) + epsilon)
    k_hat = k_raw * k_scale
    k_norm = (k_hat * kg_in[...]).astype(BF16)
    values = key_value[:, head_dim:].astype(BF16)
    for h in range(heads // 2):
        pair = pl.ds(h * 2 * cap, 2 * cap)
        expo = jnp.exp(dot(k_norm, q_sel_t[:, pair]) * scale) * allowed[...]
        total = jnp.sum(expo, axis=0, keepdims=True)
        probs = expo * (1.0 / jnp.where(total > 0.0, total, 1.0))
        probs_b = probs.astype(BF16)
        probs_all[:, pair] = probs_b
        dprob = dot(values, c_sel_t[:, pair])
        delta = jnp.sum(probs_b.astype(F32) * dprob, axis=0, keepdims=True)
        dscore_all[:, pair] = (probs * (dprob - delta) * scale).astype(BF16)
    d_key = dot(dscore_all[...], q_sel[...])
    d_value = dot(probs_all[...], c_sel[...])
    d_khat = d_key * kg_in[...]
    d_kraw = k_scale * (d_khat - k_hat * jnp.mean(d_khat * k_hat, axis=-1, keepdims=True))
    d_kv[0, :, :head_dim] = d_kraw.astype(BF16)
    d_kv[0, :, head_dim:] = d_value.astype(BF16)
    swap_d = remote(d_kv.at[0], d_kv.at[1], core_sem.at[2], core_sem.at[3], sibling)
    swap_d.start()
    gain = jnp.sum(d_key * k_hat, axis=0, keepdims=True)
    gain_core[0] = jnp.broadcast_to(gain, (8, head_dim))
    swap_g = remote(gain_core.at[0], gain_core.at[1], core_sem.at[4], core_sem.at[5], sibling)
    swap_g.start()
    parts = []
    mids = {}
    nears = {}
    columns = []
    gains = []

    def begin(copy):
        copy.start()
        parts.append(copy)
        return copy

    def make(k):
        target = chip_at(k)
        block = pl.ds(pl.multiple_of(target * rows, 128), rows)
        if k == 1:
            mixed = dot(hid_t[block, :length], d_kv[0])
            swap_d.wait()
            part[target] = (mixed + dot(hid_t[block, length:], d_kv[1])).astype(BF16)
        else:
            part[target] = dot(hid_t[block, :], d_kv[...].reshape(2 * length, 2 * half)).astype(BF16)
        for s in range(1, tall):
            for t in range(1, wide):
                share_of = rows_of(place(s, t))
                mids[k, 0, s, t] = begin(
                    remote(
                        part.at[target, share_of, low],
                        mid_row.at[k - 1, s, t],
                        mid_row_sem.at[0, k - 1, s - 1, t - 1],
                        mid_row_sem.at[1, k - 1, s - 1, t - 1],
                        to_data(place(0, t)),
                    )
                )
                mids[k, 1, s, t] = begin(
                    remote(
                        part.at[target, share_of, high],
                        mid_col.at[k - 1, s, t],
                        mid_col_sem.at[0, k - 1, s - 1, t - 1],
                        mid_col_sem.at[1, k - 1, s - 1, t - 1],
                        to_data(place(s, 0)),
                    )
                )
        for t in range(1, wide):
            whole = tall == 1
            nears[k, 0, t, 0] = begin(
                remote(
                    part.at[target, rows_of(place(0, t))] if whole else part.at[target, rows_of(place(0, t)), low],
                    from_row.at[t, k - 1] if whole else from_row.at[t, k - 1, :, low],
                    row_sem.at[0, 0, k - 1, t - 1],
                    row_sem.at[1, 0, k - 1, t - 1],
                    to_data(place(0, t)),
                )
            )
        for s in range(1, tall):
            nears[k, s, 0, 1] = begin(
                remote(
                    part.at[target, rows_of(place(s, 0)), high],
                    from_col.at[s, k - 1, :, high],
                    col_sem.at[0, 0, k - 1, s - 1],
                    col_sem.at[1, 0, k - 1, s - 1],
                    to_data(place(s, 0)),
                )
            )

    def relay(k):
        target = chip_at(k)
        for s in range(1, tall):
            sent = part[target, rows_of(place(s, 0)), low].astype(F32)
            for t in range(1, wide):
                mids[k, 0, s, t].wait_recv()
                sent += mid_row[k - 1, s, t].astype(F32)
            relay_col[k - 1, s] = sent.astype(BF16)
            nears[k, s, 0, 0] = begin(
                remote(
                    relay_col.at[k - 1, s],
                    from_col.at[s, k - 1, :, low],
                    col_sem.at[0, 1, k - 1, s - 1],
                    col_sem.at[1, 1, k - 1, s - 1],
                    to_data(place(s, 0)),
                )
            )
        if tall == 1:
            return
        for t in range(1, wide):
            sent = part[target, rows_of(place(0, t)), high].astype(F32)
            for s in range(1, tall):
                mids[k, 1, s, t].wait_recv()
                sent += mid_col[k - 1, s, t].astype(F32)
            relay_row[k - 1, t] = sent.astype(BF16)
            nears[k, 0, t, 1] = begin(
                remote(
                    relay_row.at[k - 1, t],
                    from_row.at[t, k - 1, :, high],
                    row_sem.at[0, 1, k - 1, t - 1],
                    row_sem.at[1, 1, k - 1, t - 1],
                    to_data(place(0, t)),
                )
            )

    def collect(k):
        target = chip_at(k)
        for key in nears:
            if key[0] == k:
                nears[key].wait_recv()
        total = part[target, mine].astype(F32)
        for s in range(1, tall):
            total += from_col[s, k - 1].astype(F32)
        for t in range(1, wide):
            total += from_row[t, k - 1].astype(F32)
        if k < chips:
            z_out[k] = total.astype(BF16)
            copy = remote(z_out.at[k], from_z.at[k], z_sem.at[0, k], z_sem.at[1, k], to_chip(target))
            copy.start()
            columns.append(copy)
        return total

    for k in range(1, chips + 3):
        if k <= chips:
            make(k)
        if k == 1:
            swap_g.wait()
            gain_data[dp] = gain_core[0] + gain_core[1]
            for d in range(1, data):
                copy = remote(
                    gain_data.at[dp], gain_data.at[dp], gain_data_sem.at[0, d], gain_data_sem.at[1, d], to_data(data_at(d))
                )
                copy.start()
                gains.append(copy)
        if 1 <= k - 1 <= chips:
            relay(k - 1)
        if 1 <= k - 2 <= chips:
            summed = collect(k - 2)

    for copy in gains:
        copy.wait()
    gain_sum = gain_data[0]
    for d in range(1, data):
        gain_sum += gain_data[d]
    gain_z[chip] = gain_sum
    z_gains = []
    for k in range(1, chips):
        copy = remote(
            gain_z.at[chip], gain_z.at[chip], gain_z_sem.at[0, k], gain_z_sem.at[1, k], to_chip(chip_at(k))
        )
        copy.start()
        z_gains.append(copy)

    for k in range(1, chips):
        columns[k - 1].wait_recv()
        summed += from_z[k].astype(F32)
    final[mine] = summed.astype(BF16)
    finals = []
    for d in range(1, data):
        copy = remote(final.at[mine], final.at[mine], final_sem.at[0, d], final_sem.at[1, d], to_data(data_at(d)))
        copy.start()
        finals.append(copy)

    for copy in z_gains:
        copy.wait()
    gain_sum = gain_z[0]
    for k in range(1, chips):
        gain_sum += gain_z[k]
    d_gain[...] = gain_sum

    for copy in sends + ahead + parts + columns:
        copy.wait_send()
    for copy in finals:
        copy.wait()
    d_weight[...] = final[...]


def widen(narrow, gain, d_weight, d_gain):
    d_weight[...] = narrow[: d_weight.shape[0]].astype(F32)
    d_gain[...] = gain[0]


def shards(grid, owners, hidden, queries, upstream, advantage, selected, segment, w_kv, k_gain, q_gain):
    hidden_row = hidden[0]
    length, width = hidden_row.shape
    rows_dev, columns = w_kv.shape
    head_dim = k_gain.shape[0]
    heads = queries.shape[2] // head_dim
    tall, wide = grid
    data = tall * wide
    far = (2, owners // 2, tall - 1, wide - 1) if tall > 1 else (2, 1, 1, 1)
    unit = math.lcm(128, 16 * data)
    rows = -(-rows_dev // unit) * unit
    chips = owners // 2
    share = rows // data
    if rows_dev * owners != width:
        hidden_row = jnp.pad(hidden_row, ((0, 0), (0, rows_dev * owners - width)))
    if rows != rows_dev:
        blocks = hidden_row.reshape(length, owners, rows_dev)
        hidden_row = jnp.pad(blocks, ((0, 0), (0, 0), (0, rows - rows_dev))).reshape(length, owners * rows)
        w_kv = jnp.pad(w_kv, ((0, rows - rows_dev), (0, 0)))
    vmem = pl.BlockSpec(memory_space=pltpu.VMEM)
    hbm = pl.BlockSpec(memory_space=pltpu.HBM)
    dma = pltpu.SemaphoreType.DMA
    d_weight, d_gain = pl.pallas_call(
        functools.partial(body, grid, owners),
        out_shape=(
            jax.ShapeDtypeStruct((rows, columns), BF16),
            jax.ShapeDtypeStruct((8, head_dim), F32),
        ),
        in_specs=[hbm] * 9,
        out_specs=(vmem, vmem),
        scratch_shapes=[
            pltpu.VMEM((1, length), F32),
            pltpu.VMEM((1, length), jnp.int32),
            pltpu.VMEM((1, length), jnp.int32),
            pltpu.VMEM((1, head_dim), F32),
            pltpu.VMEM((1, head_dim), F32),
            pltpu.VMEM((2, length, chips * rows), BF16),
            pltpu.VMEM((chips * rows, 2 * length), BF16),
            pltpu.VMEM((chips, rows, columns), BF16),
            pltpu.VMEM((length, heads * head_dim), BF16),
            pltpu.VMEM((length, heads * head_dim), BF16),
            pltpu.VMEM((heads * CAP, head_dim), BF16),
            pltpu.VMEM((heads * CAP, head_dim), BF16),
            pltpu.VMEM((head_dim, heads * CAP), BF16),
            pltpu.VMEM((head_dim, heads * CAP), BF16),
            pltpu.VMEM((length, heads * CAP), BF16),
            pltpu.VMEM((length, heads * CAP), BF16),
            pltpu.VMEM((length, 2 * CAP), F32),
            pltpu.VMEM((length, columns), F32),
            pltpu.VMEM((length, columns), F32),
            pltpu.VMEM((length, columns), F32),
            pltpu.VMEM((2, length, columns), BF16),
            pltpu.VMEM((chips, rows, columns), BF16),
            pltpu.VMEM((chips, tall, wide, share, columns // 2), BF16),
            pltpu.VMEM((chips, tall, wide, share, columns // 2), BF16),
            pltpu.VMEM((chips, wide, share, columns // 2), BF16),
            pltpu.VMEM((chips, tall, share, columns // 2), BF16),
            pltpu.VMEM((wide, chips, share, columns), BF16),
            pltpu.VMEM((tall, chips, share, columns), BF16),
            pltpu.VMEM((chips, share, columns), BF16),
            pltpu.VMEM((chips, share, columns), BF16),
            pltpu.VMEM((rows, columns), BF16),
            pltpu.VMEM((2, 8, head_dim), F32),
            pltpu.VMEM((data, 8, head_dim), F32),
            pltpu.VMEM((chips, 8, head_dim), F32),
            dma((8,)),
            dma((3, chips)),
            dma((2, chips)),
            dma((2, chips, max(wide - 1, 1))),
            dma((2, chips, max(tall - 1, 1))),
            dma(far),
            dma(far),
            dma((6,)),
            dma(far),
            dma(far),
            dma((2, 2, chips, max(wide - 1, 1))),
            dma((2, 2, chips, max(tall - 1, 1))),
            dma((2, chips)),
            dma((2, data)),
            dma((2, data)),
            dma((2, chips)),
        ],
        compiler_params=pltpu.CompilerParams(
            collective_id=0, has_side_effects=True, vmem_limit_bytes=64 * 1024 * 1024
        ),
        cost_estimate=pl.CostEstimate(flops=2_000_000_000, bytes_accessed=6_000_000, transcendentals=300_000),
        name="kv_backward",
    )(
        hidden_row,
        queries[0],
        upstream[0],
        advantage,
        selected,
        segment,
        w_kv,
        k_gain.reshape(1, head_dim),
        q_gain.reshape(1, head_dim),
    )
    return pl.pallas_call(
        widen,
        out_shape=(
            jax.ShapeDtypeStruct((rows_dev, columns), F32),
            jax.ShapeDtypeStruct((head_dim,), F32),
        ),
        in_specs=[vmem, vmem],
        out_specs=(vmem, vmem),
        compiler_params=pltpu.CompilerParams(vmem_limit_bytes=64 * 1024 * 1024),
        name="widen",
    )(d_weight, d_gain)


def solution(mesh):
    in_specs = (
        P(("dp", "fsdp"), None, None),
        P(("dp", "fsdp"), None, None),
        P(("dp", "fsdp"), None, None),
        P(("dp", "fsdp"), None),
        P(("dp", "fsdp"), None),
        P(("dp", "fsdp"), None),
        P("fsdp", None),
        P(),
        P(),
    )
    out_specs = (P("fsdp", None), P())
    data = mesh.shape["dp"]
    tall = 1
    return jax.shard_map(
        functools.partial(shards, (tall, data // tall), mesh.shape["fsdp"]),
        mesh=mesh,
        in_specs=in_specs,
        out_specs=out_specs,
        check_vma=False,
    )
```
